128 devices in a mesh: lat: 8 (over z, y_hi), lon: 16 (over x, y_lo, core).
Axes of the slice: x: 4, y: 4 (y_hi: 2, y_lo: 2; y = y_hi * 2 + y_lo), z: 4, core: 2. Of those that a mesh axis runs over, the one named last changes fastest.
Arguments:
- tokens: bfloat16 [4, 192, 384, 512], P(None, 'lat', 'lon'), may hold values from -6 to 6
- enc_gain: float32 [512], replicated, may hold values from 0.1 to 1.9
- enc_qkv: bfloat16 [512, 1536], replicated, may hold values from -0.25 to 0.25
- enc_proj: bfloat16 [512, 512], replicated, may hold values from -0.25 to 0.25
- enc_tau: float32 [8], replicated, may hold values from 4 to 20
- merge_gain: float32 [2048], replicated, may hold values from 0.1 to 1.9
- merge_weight: bfloat16 [2048, 1024], replicated, may hold values from -0.125 to 0.125
- coarse_gain: float32 [1024], replicated, may hold values from 0.1 to 1.9
- coarse_qkv: bfloat16 [1024, 3072], P('lon'), may hold values from -0.1875 to 0.1875
- coarse_proj: bfloat16 [1024, 1024], P('lon'), may hold values from -0.1875 to 0.1875
- coarse_tau: float32 [16], replicated, may hold values from 4 to 20
- expand_weight: bfloat16 [1024, 2048], replicated, may hold values from -0.1875 to 0.1875
- dec_gain: float32 [512], replicated, may hold values from 0.1 to 1.9
- dec_qkv: bfloat16 [512, 1536], replicated, may hold values from -0.25 to 0.25
- dec_proj: bfloat16 [512, 512], replicated, may hold values from -0.25 to 0.25
- dec_tau: float32 [8], replicated, may hold values from 4 to 20
Outputs:
- decoded: bfloat16 [4, 192, 384, 512], P(None, 'lat', 'lon')
The draws below stay inside these ranges and needn't reach their ends.
All inputs are finite; a program needn't handle non-finite values.
Results may differ from the reference program's by a relative error of at most 0.025.
Values may be sent and summed in bfloat16 or wider, within the bound.
A program may use at most 128 MiB of HBM per device.

```python
import math
import jax
import jax.numpy as jnp
from jax import lax

D1 = 512
D2 = 1024
H1 = 8
H2 = 16
LEV = 4
NLAT = 192
NLON = 384


def block_scale(stream_key, extent, pieces, low, high):
    def one(axis_at, parts):
        draws = jax.random.uniform(jax.random.fold_in(jax.random.fold_in(stream_key, 6), axis_at), (parts,), jnp.float32, low / len(pieces), high / len(pieces))
        return jnp.repeat(jnp.exp(draws), extent[axis_at] // parts).reshape((-1,) + (1,) * (len(extent) - axis_at - 1))

    loudness = one(*pieces[0])
    for cut in pieces[1:]:
        loudness = loudness * one(*cut)
    return loudness


def gaussian(key, shape, scale, bound, split=(), dtype=jnp.bfloat16):
    loudness = block_scale(key, shape, split, -0.22, 0.18) if split else 1.0
    array = jax.random.normal(key, shape, jnp.float32) * scale * loudness
    return jnp.minimum(jnp.maximum(array, -bound), bound).astype(dtype)


def setup_inputs(seed: int = 0) -> dict:
    splits = jax.random.split(jax.random.key(seed), 17)
    tokens = gaussian(splits[0], (LEV, NLAT, NLON, D1), 1.0, 6.0, ((1, 8), (2, 16)))
    enc_gain = jnp.clip(1.0 + 0.18 * jax.random.normal(splits[1], (D1,), jnp.float32), 0.1, 1.9)
    enc_qkv = gaussian(splits[2], (D1, 3 * D1), D1 ** -0.5, 0.25)
    enc_proj = gaussian(splits[3], (D1, D1), D1 ** -0.5, 0.25)
    enc_tau = jnp.clip(jnp.exp(jax.random.uniform(splits[4], (H1,), jnp.float32, math.log(4.0), math.log(20.0))), 4.0, 20.0)
    merge_gain = jnp.clip(1.0 + 0.18 * jax.random.normal(splits[5], (4 * D1,), jnp.float32), 0.1, 1.9)
    merge_weight = gaussian(splits[6], (4 * D1, D2), (4 * D1) ** -0.5, 0.125)
    coarse_gain = jnp.clip(1.0 + 0.18 * jax.random.normal(splits[7], (D2,), jnp.float32), 0.1, 1.9)
    coarse_qkv = gaussian(splits[8], (D2, 3 * D2), D2 ** -0.5, 0.1875, ((0, 16),))
    coarse_proj = gaussian(splits[9], (D2, D2), D2 ** -0.5, 0.1875, ((0, 16),))
    coarse_tau = jnp.clip(jnp.exp(jax.random.uniform(splits[10], (H2,), jnp.float32, math.log(4.0), math.log(20.0))), 4.0, 20.0)
    expand_weight = gaussian(splits[11], (D2, 4 * D1), D2 ** -0.5, 0.1875)
    dec_gain = jnp.clip(1.0 + 0.18 * jax.random.normal(splits[12], (D1,), jnp.float32), 0.1, 1.9)
    dec_qkv = gaussian(splits[13], (D1, 3 * D1), D1 ** -0.5, 0.25)
    dec_proj = gaussian(splits[14], (D1, D1), D1 ** -0.5, 0.25)
    dec_tau = jnp.clip(jnp.exp(jax.random.uniform(splits[15], (H1,), jnp.float32, math.log(4.0), math.log(20.0))), 4.0, 20.0)
    return {"tokens": tokens, "enc_gain": enc_gain, "enc_qkv": enc_qkv, "enc_proj": enc_proj, "enc_tau": enc_tau, "merge_gain": merge_gain, "merge_weight": merge_weight, "coarse_gain": coarse_gain, "coarse_qkv": coarse_qkv, "coarse_proj": coarse_proj, "coarse_tau": coarse_tau, "expand_weight": expand_weight, "dec_gain": dec_gain, "dec_qkv": dec_qkv, "dec_proj": dec_proj, "dec_tau": dec_tau}


def norm_rows(values, gain):
    floats = values.astype(jnp.float32)
    center = floats - lax.optimization_barrier(jnp.mean(floats, axis=-1, keepdims=True))
    spread = lax.optimization_barrier(jnp.mean(center * center, axis=-1, keepdims=True))
    return (center * lax.rsqrt(spread + 1e-05) * gain.astype(jnp.float32)).astype(jnp.bfloat16)

def to_windows(values):
    levels, rows, columns, width = values.shape
    blocks = values.reshape(levels // 2, 2, rows // 12, 12, columns // 6, 6, width)
    return blocks.transpose(2, 0, 4, 1, 3, 5, 6).reshape(rows // 12, levels // 2 * (columns // 6), 144, width)

def from_windows(blocks, levels, rows, columns):
    width = blocks.shape[-1]
    layout = blocks.reshape(rows // 12, levels // 2, columns // 6, 2, 12, 6, width)
    return layout.transpose(1, 3, 0, 4, 2, 5, 6).reshape(levels, rows, columns, width)

def unit_rows(values):
    floats = values.astype(jnp.float32)
    return (floats * lax.rsqrt(lax.optimization_barrier(jnp.sum(floats * floats, axis=-1, keepdims=True)) + 1e-06)).astype(jnp.bfloat16)

def window_core(item, temper, heads):
    block, codes = item
    number = block.shape[0]
    width = block.shape[-1] // 3
    parted = block.reshape(number, 144, 3, heads, width // heads)
    queries = unit_rows(parted[:, :, 0])
    keyset = unit_rows(parted[:, :, 1])
    valueset = parted[:, :, 2]
    scores = jnp.einsum('wqhd,wkhd->whqk', queries, keyset, preferred_element_type=jnp.float32)
    factor = temper.astype(jnp.float32)[None, :, None, None]
    allowed = (codes[:, :, None] == codes[:, None, :])[:, None]
    weights = jnp.where(allowed, jnp.exp(factor * scores - factor), jnp.zeros_like(scores))
    chances = (weights / lax.optimization_barrier(jnp.sum(weights, axis=-1, keepdims=True))).astype(jnp.bfloat16)
    mixed = jnp.einsum('whqk,wkhd->wqhd', chances, valueset, preferred_element_type=jnp.float32)
    return mixed.astype(jnp.bfloat16).reshape(number, 144, width)

def attend(packed, codes, temper, heads):
    levels, rows, columns, _ = packed.shape
    blocks = to_windows(packed)
    code_blocks = to_windows(codes[..., None])[..., 0]
    mixed = lax.map(lambda item: window_core(item, temper, heads), (blocks, code_blocks))
    return from_windows(mixed, levels, rows, columns)

def project(values, weight):
    shape = values.shape
    product = jnp.dot(values.reshape(-1, shape[-1]), weight, preferred_element_type=jnp.float32)
    return product.reshape(shape[:-1] + (weight.shape[1],))

def region_codes(levels, rows, columns, lat_flags):
    level_flags = (jnp.arange(levels) + 1 >= levels).astype(jnp.int32)
    codes = level_flags[:, None] * 2 + lat_flags[None, :]
    return jnp.broadcast_to(codes[:, :, None], (levels, rows, columns)).astype(jnp.int32)

def merge_cells(layout):
    levels, rows, columns, width = layout.shape
    parted = layout.reshape(levels, rows // 2, 2, columns // 2, 2, width)
    return parted.transpose(0, 1, 3, 2, 4, 5).reshape(levels, rows // 2, columns // 2, 4 * width)

def split_cells(coarse):
    levels, rows, columns, wide = coarse.shape
    parted = coarse.reshape(levels, rows, columns, 2, 2, wide // 4)
    return parted.transpose(0, 1, 3, 2, 4, 5).reshape(levels, 2 * rows, 2 * columns, wide // 4)

def fine_block(layout, gain, weight_qkv, weight_proj, temper, heads):
    levels, rows, columns, width = layout.shape
    normed = norm_rows(layout, gain)
    rolled = jnp.roll(normed, (-1, -6, -3), (0, 1, 2))
    packed = project(rolled, weight_qkv).astype(jnp.bfloat16)
    lat_flags = (jnp.arange(rows) + 6 >= rows).astype(jnp.int32)
    mixed = attend(packed, region_codes(levels, rows, columns, lat_flags), temper, heads)
    shifted = project(mixed, weight_proj).astype(jnp.bfloat16)
    back = jnp.roll(shifted, (1, 6, 3), (0, 1, 2))
    return (layout.astype(jnp.float32) + back.astype(jnp.float32)).astype(jnp.bfloat16)

def reference(tokens, enc_gain, enc_qkv, enc_proj, enc_tau, merge_gain, merge_weight, coarse_gain, coarse_qkv, coarse_proj, coarse_tau, expand_weight, dec_gain, dec_qkv, dec_proj, dec_tau):
    encoded = fine_block(tokens, enc_gain, enc_qkv, enc_proj, enc_tau, H1)
    coarse = project(norm_rows(merge_cells(encoded), merge_gain), merge_weight).astype(jnp.bfloat16)
    packed = project(norm_rows(coarse, coarse_gain), coarse_qkv).astype(jnp.bfloat16)
    levels, rows, columns, _ = coarse.shape
    mixed = attend(packed, jnp.zeros((levels, rows, columns), jnp.int32), coarse_tau, H2)
    coarse_out = (coarse.astype(jnp.float32) + project(mixed, coarse_proj)).astype(jnp.bfloat16)
    expanded = split_cells(project(coarse_out, expand_weight).astype(jnp.bfloat16))
    joined = (encoded.astype(jnp.float32) + expanded.astype(jnp.float32)).astype(jnp.bfloat16)
    return fine_block(joined, dec_gain, dec_qkv, dec_proj, dec_tau, H1)
```

```python
import functools

import jax
import jax.numpy as jnp
import numpy as np
from jax import lax
from jax.experimental import pallas as pl
from jax.experimental.pallas import tpu as pltpu
from jax.sharding import PartitionSpec as P

MESH = pl.DeviceIdType.MESH
BF = jnp.bfloat16
F32 = jnp.float32
LOG2E = 1.4426950408889634
NT = (((1,), (1,)), ((), ()))
ANY = pl.BlockSpec(memory_space=pl.ANY)
VMEM = pl.BlockSpec(memory_space=pltpu.VMEM)
SMEM = pl.BlockSpec(memory_space=pltpu.SMEM)


def dot(a, b):
    return jnp.dot(a, b, preferred_element_type=F32)


def beside_at(level, row, column):
    return (row // 2) * 16 + level * 6 + (row % 2) * 3 + column


def block_to_windows():
    table = np.zeros((192, 224), np.float32)
    for w in range(4):
        for level in range(2):
            for row in range(4):
                for c in range(6):
                    column = 3 + 6 * w + c
                    if column < 24:
                        source = level * 96 + row * 24 + column
                    else:
                        source = 192 + beside_at(level, row, column - 24)
                    table[w * 48 + level * 24 + row * 6 + c, source] = 1
    return table


def beside_to_block():
    table = np.zeros((192, 32), np.float32)
    for level in range(2):
        for row in range(4):
            for c in range(3):
                table[level * 96 + row * 24 + c, beside_at(level, row, c)] = 1
    return table


def block_row(block, row):
    if block < 4:
        return 6 + 4 * block + row
    if block == 4:
        return 22 + row if row < 2 else row - 2
    return 2 + row


def grid_to_beside():
    table = np.zeros((2, 192, 576), np.float32)
    for block in range(6):
        for level in range(2):
            for row in range(4):
                for c in range(3):
                    at = block * 32 + beside_at(level, row, c)
                    table[level, at, block_row(block, row) * 24 + c] = 1
    return table


def grid_to_cells():
    table = np.zeros((384, 384), np.float32)
    for pr in range(2):
        for pc in range(2):
            for cw in range(2):
                for level in range(2):
                    for i in range(4):
                        for j in range(6):
                            at = (pr * 2 + pc) * 96 + cw * 48 + level * 24 + i * 6 + j
                            source = level * 192 + (2 * i + pr) * 24 + 2 * (6 * cw + j) + pc
                            table[at, source] = 1
    return table


def differences():
    token = np.arange(144)
    level = (token // 24) % 2
    low = ((token // 48) * 4 + (token % 24) // 6) >= 6
    keys = np.concatenate([token[:128], np.tile(token[128:], 8)])
    by_level = (level[:, None] != level[keys][None]).astype(np.float32)
    by_row = (low[:, None] != low[keys][None]).astype(np.float32)
    return np.stack([by_level, by_row]) * np.float32(-1e30)


def half_masks():
    left = np.zeros((2, 128, 128), np.float32)
    left[0, :, :64] = 1
    left[1, :, 64:] = 1
    return left


def tail_mask():
    return (np.arange(128)[:, None] // 16 == np.arange(512)[None] // 64).astype(np.float32)


def head_sums():
    at = np.arange(256) // 64
    return (at[:, None] == at[None]).astype(np.float32)


def norm_block(values, gain):
    mean = jnp.mean(values, axis=-1, keepdims=True)
    center = values - mean
    spread = jnp.mean(center * center, axis=-1, keepdims=True)
    return (center * lax.rsqrt(spread + 1e-05) * gain).astype(BF)


def head_scale(tau_ref, first):
    at = lax.broadcasted_iota(jnp.int32, (1, 256), 1) // 64
    scale = jnp.full((1, 256), tau_ref[first], F32)
    for h in range(1, 4):
        scale = jnp.where(at == h, tau_ref[first + h], scale)
    return scale * LOG2E


def make_qkv(x_ref, w_ref, q_ref, k_ref, v_ref, tau_ref, sums, width, group, depth):
    for half in range(2):
        at = group * 512 + half * 256
        lanes = slice(half * 256, half * 256 + 256)
        for part, target in ((0, q_ref), (1, k_ref)):
            product = dot(x_ref[...], w_ref[:, part * width + at : part * width + at + 256])
            rounded = product.astype(BF)
            total = dot(rounded * rounded, sums)
            factor = lax.rsqrt(total + 1e-06)
            if part == 0:
                factor = factor * head_scale(tau_ref, group * 8 + half * 4)
            target[:, lanes] = (product * factor).astype(BF)
        product = dot(x_ref[...], w_ref[:, 2 * width + at : 2 * width + at + 256])
        v_ref[:, lanes] = product.astype(BF)


def attend(q_ref, k_ref, v_ref, out_ref, out_at, bias_ref, masks_ref, tail_ref):
    def one_window(w, carry):
        row = pl.multiple_of(w * 144, 16)
        q = q_ref[pl.ds(row, 144), :]
        tail = tail_ref[...]
        left, right = masks_ref[0], masks_ref[1]
        k_tail = k_ref[pl.ds(pl.multiple_of(row + 128, 16), 16), :]
        v_tail = v_ref[pl.ds(pl.multiple_of(row + 128, 16), 16), :]
        k_tails = jnp.concatenate([k_tail] * 8, axis=0) * tail
        v_tails = jnp.concatenate([v_tail] * 8, axis=0) * tail
        score = lax.dot_general(q, k_tails, NT, preferred_element_type=F32)
        if bias_ref is not None:
            score = score + bias_ref[:, 128:]
        p_tail = jnp.exp2(score).astype(BF)
        for pair in range(4):
            lanes = slice(pair * 128, pair * 128 + 128)
            k = k_ref[pl.ds(row, 128), lanes]
            v = v_ref[pl.ds(row, 128), lanes]
            k_pair = jnp.concatenate([k * left, k * right], axis=0)
            score = lax.dot_general(q[:, lanes], k_pair, NT, preferred_element_type=F32)
            if bias_ref is not None:
                bias = bias_ref[:, :128]
                score = score + jnp.concatenate([bias, bias], axis=1)
            weight = jnp.exp2(score).astype(BF)
            v_pair = jnp.concatenate(
                [
                    jnp.concatenate([v * left, left], axis=1),
                    jnp.concatenate([v * right, right], axis=1),
                ],
                axis=0,
            )
            v_end = jnp.concatenate([v_tails[:, lanes], tail[:, lanes]], axis=1)
            both = dot(weight, v_pair) + dot(p_tail, v_end)
            mixed = (both[:, :128] / both[:, 128:]).astype(BF)
            out_ref[pl.ds(row, 144), pl.ds(out_at + pair * 128, 128)] = mixed
        return carry

    lax.fori_loop(0, 4, one_window, 0)


def fine_kernel(
    lat_size,
    lon_size,
    tokens,
    gain_ref,
    w_qkv,
    w_proj,
    tau_ref,
    to_windows,
    from_windows,
    spread_ref,
    pick_ref,
    diff_ref,
    masks_ref,
    tail_ref,
    sums_ref,
    out_hbm,
    grid,
    blocks,
    picked,
    wq,
    wp,
    x_ref,
    q_ref,
    k_ref,
    v_ref,
    mixed_ref,
    shifted_ref,
    bias_ref,
    row_out,
    col_out,
    row_in,
    col_in,
    local_sem,
    send_sem,
    recv_sem,
    back_send,
    back_recv,
):
    lat, lon = lax.axis_index("lat"), lax.axis_index("lon")
    up, down = lax.rem(lat + lat_size - 1, lat_size), lax.rem(lat + 1, lat_size)
    west, east = lax.rem(lon + lon_size - 1, lon_size), lax.rem(lon + 1, lon_size)
    levels = ((1, 2), (3, 0))

    load = pltpu.make_async_copy(tokens, grid, local_sem.at[0])
    load.start()
    load_q = pltpu.make_async_copy(w_qkv, wq, local_sem.at[1])
    load_q.start()
    load_p = pltpu.make_async_copy(w_proj, wp, local_sem.at[2])
    load_p.start()
    own = []
    for g in range(2):
        for side in range(2):
            level = levels[g][side]
            for b in range(5):
                size = 96 if b < 4 else 48
                copy = pltpu.make_async_copy(
                    tokens.at[level, pl.ds(144 + 96 * b, size)],
                    blocks.at[g, b, pl.ds(96 * side, size)],
                    local_sem.at[3 + (g * 2 + side) * 5 + b],
                )
                copy.start()
                own.append(copy)

    barrier = pltpu.get_barrier_semaphore()
    for device in ((up, lon), (down, lon), (lat, west), (lat, east), (up, west), (down, east)):
        pl.semaphore_signal(barrier, inc=1, device_id=device, device_id_type=MESH)
    pl.semaphore_wait(barrier, 6)

    def send(source, target, sems, at, device):
        copy = pltpu.make_async_remote_copy(
            src_ref=source,
            dst_ref=target,
            send_sem=sems[0].at[at],
            recv_sem=sems[1].at[at],
            device_id=device,
            device_id_type=MESH,
        )
        copy.start()
        return copy

    there = (send_sem, recv_sem)
    rows = {}
    columns = {}

    def send_rows(g):
        for side in range(2):
            level = levels[g][side]
            at = g * 8 + side * 2
            rows[g, side, 0] = send(
                tokens.at[level, pl.ds(0, 48)],
                blocks.at[g, 4, pl.ds(96 * side + 48, 48)],
                there,
                at,
                (up, lon),
            )
            rows[g, side, 1] = send(
                tokens.at[level, pl.ds(48, 96)],
                blocks.at[g, 5, pl.ds(96 * side, 96)],
                there,
                at + 1,
                (up, lon),
            )

    def send_columns(g):
        picks = dot(pick_ref[0], grid[levels[g][0]]) + dot(pick_ref[1], grid[levels[g][1]])
        for b in range(6):
            picked[g, b] = picks[32 * b : 32 * b + 32].astype(BF)
        at = g * 8 + 4
        columns[g, 0] = send(
            picked.at[g, pl.ds(0, 4)],
            blocks.at[g, pl.ds(0, 4), pl.ds(192, 32)],
            there,
            at,
            (lat, west),
        )
        columns[g, 1] = send(
            picked.at[g, 4, pl.ds(0, 16)],
            blocks.at[g, 4, pl.ds(192, 16)],
            there,
            at + 1,
            (lat, west),
        )
        columns[g, 2] = send(
            picked.at[g, 4, pl.ds(16, 16)],
            blocks.at[g, 4, pl.ds(208, 16)],
            there,
            at + 2,
            (up, west),
        )
        columns[g, 3] = send(
            picked.at[g, 5], blocks.at[g, 5, pl.ds(192, 32)], there, at + 3, (up, west)
        )

    send_rows(0)
    load.wait()
    send_columns(0)
    send_columns(1)
    send_rows(1)
    load_q.wait()
    load_p.wait()
    for copy in own:
        copy.wait()

    back = (back_send, back_recv)
    backs = {}
    last = (lat == lat_size - 1).astype(F32)

    def add_rows(level, at, size, values):
        grid[level, pl.ds(at, size), :] = (
            grid[level, pl.ds(at, size), :].astype(F32) + values
        ).astype(BF)

    for g in range(2):
        for half in range(2):
            if half == 0:
                columns[g, 0].wait_recv()
            else:
                for part in (1, 2, 3):
                    columns[g, part].wait_recv()
                for side in range(2):
                    rows[g, side, 0].wait_recv()
                    rows[g, side, 1].wait_recv()
            gain = gain_ref[...]
            for b in range(3):
                tokens_in = dot(to_windows[...], blocks[g, 3 * half + b])
                normed = norm_block(tokens_in, gain)
                for w in range(4):
                    x_ref[w * 144 + b * 48 : w * 144 + b * 48 + 48, :] = normed[
                        48 * w : 48 * w + 48
                    ]
            make_qkv(x_ref, wq, q_ref, k_ref, v_ref, tau_ref, sums_ref[...], 512, 0, 512)
            masked = g == 1 or half == 1
            if masked:
                bias = jnp.zeros((144, 256), F32)
                if g == 1:
                    bias = bias + diff_ref[0]
                if half == 1:
                    bias = bias + diff_ref[1] * last
                bias_ref[...] = bias
            attend(
                q_ref,
                k_ref,
                v_ref,
                mixed_ref,
                0,
                bias_ref if masked else None,
                masks_ref,
                tail_ref,
            )
            shifted_ref[...] = dot(mixed_ref[...], wp[...]).astype(BF)
            for b in range(3):
                index = 3 * half + b
                parts = [
                    shifted_ref[w * 144 + b * 48 : w * 144 + b * 48 + 48, :] for w in range(4)
                ]
                placed = dot(from_windows[...], jnp.concatenate(parts, axis=0))
                col_out[g, index] = placed[192:224].astype(BF)
                for side in range(2):
                    level = levels[g][side]
                    mine = placed[96 * side : 96 * side + 96]
                    if index < 4:
                        add_rows(level, 144 + 96 * index, 96, mine)
                    elif index == 4:
                        add_rows(level, 528, 48, mine[:48])
                        row_out[g, 48 * side : 48 * side + 48, :] = mine[48:].astype(BF)
                    else:
                        row_out[g, 96 + 96 * side : 192 + 96 * side, :] = mine.astype(BF)
            at = g * 6
            if half == 1:
                backs[g, 0] = send(row_out.at[g], row_in.at[g], back, at, (down, lon))
                backs[g, 1] = send(
                    col_out.at[g, pl.ds(0, 4)],
                    col_in.at[g, pl.ds(0, 4)],
                    back,
                    at + 1,
                    (lat, east),
                )
                backs[g, 2] = send(
                    col_out.at[g, 4, pl.ds(0, 16)],
                    col_in.at[g, 4, pl.ds(0, 16)],
                    back,
                    at + 2,
                    (lat, east),
                )
                backs[g, 3] = send(
                    col_out.at[g, 4, pl.ds(16, 16)],
                    col_in.at[g, 4, pl.ds(16, 16)],
                    back,
                    at + 3,
                    (down, east),
                )
                backs[g, 4] = send(
                    col_out.at[g, 5], col_in.at[g, 5], back, at + 4, (down, east)
                )

    for g in range(2):
        for part in range(1, 5):
            backs[g, part].wait_recv()
        for b in range(4):
            placed = dot(spread_ref[...], col_in[g, b])
            for side in range(2):
                add_rows(levels[g][side], 144 + 96 * b, 96, placed[96 * side : 96 * side + 96])
        backs[g, 0].wait_recv()
        placed = dot(spread_ref[...], col_in[g, 4])
        for side in range(2):
            mine = placed[96 * side : 96 * side + 96]
            add_rows(levels[g][side], 528, 48, mine[:48])
            above = row_in[g, 48 * side : 48 * side + 48, :].astype(F32)
            add_rows(levels[g][side], 0, 48, mine[48:] + above)
        placed = dot(spread_ref[...], col_in[g, 5])
        for side in range(2):
            above = row_in[g, 96 + 96 * side : 192 + 96 * side, :].astype(F32)
            add_rows(levels[g][side], 48, 96, placed[96 * side : 96 * side + 96] + above)

    store = pltpu.make_async_copy(grid, out_hbm, local_sem.at[0])
    store.start()
    for copy in (*rows.values(), *columns.values(), *backs.values()):
        copy.wait_send()
    store.wait()


def fine_block(grid, gain, w_qkv, w_proj, tau, tables, name, number):
    kernel = functools.partial(fine_kernel, lax.axis_size("lat"), lax.axis_size("lon"))
    return pl.pallas_call(
        kernel,
        out_shape=jax.ShapeDtypeStruct((4, 576, 512), BF),
        in_specs=[ANY, VMEM, ANY, ANY, SMEM] + [VMEM] * 8,
        out_specs=ANY,
        scratch_shapes=[
            pltpu.VMEM((4, 576, 512), BF),
            pltpu.VMEM((2, 6, 224, 512), BF),
            pltpu.VMEM((2, 6, 32, 512), BF),
            pltpu.VMEM((512, 1536), BF),
            pltpu.VMEM((512, 512), BF),
            pltpu.VMEM((576, 512), BF),
            pltpu.VMEM((576, 512), BF),
            pltpu.VMEM((576, 512), BF),
            pltpu.VMEM((576, 512), BF),
            pltpu.VMEM((576, 512), BF),
            pltpu.VMEM((576, 512), BF),
            pltpu.VMEM((144, 256), F32),
            pltpu.VMEM((2, 288, 512), BF),
            pltpu.VMEM((2, 6, 32, 512), BF),
            pltpu.VMEM((2, 288, 512), BF),
            pltpu.VMEM((2, 6, 32, 512), BF),
            pltpu.SemaphoreType.DMA((23,)),
            pltpu.SemaphoreType.DMA((16,)),
            pltpu.SemaphoreType.DMA((16,)),
            pltpu.SemaphoreType.DMA((12,)),
            pltpu.SemaphoreType.DMA((12,)),
        ],
        compiler_params=pltpu.CompilerParams(
            collective_id=number, has_side_effects=True, vmem_limit_bytes=40 << 20
        ),
        cost_estimate=pl.CostEstimate(
            flops=12_000_000_000, bytes_accessed=8_000_000, transcendentals=3_000_000
        ),
        name=name,
    )(grid, gain.reshape(1, 512), w_qkv, w_proj, tau, *tables)


def coarse_kernel(
    encoded,
    merge_gain,
    merge_weight,
    gain_ref,
    w_qkv,
    w_proj,
    tau_ref,
    w_split,
    to_cells,
    from_cells,
    masks_ref,
    tail_ref,
    sums_ref,
    out_hbm,
    grid,
    wm,
    wq,
    wp,
    ws,
    merged,
    coarse,
    x_ref,
    q_ref,
    k_ref,
    v_ref,
    mixed_ref,
    split,
    sem,
):
    loads = [
        pltpu.make_async_copy(source, target, sem.at[i])
        for i, (source, target) in enumerate(
            ((encoded, grid), (merge_weight, wm), (w_qkv, wq), (w_proj, wp), (w_split, ws))
        )
    ]
    for load in loads:
        load.start()
    loads[0].wait()
    for g in range(2):
        for b in range(3):
            cells = dot(to_cells[:, :192], grid[2 * g, pl.ds(192 * b, 192), :]) + dot(
                to_cells[:, 192:], grid[2 * g + 1, pl.ds(192 * b, 192), :]
            )
            parts = [cells[96 * n : 96 * n + 96] for n in range(4)]
            mean = sum(jnp.sum(part, axis=-1, keepdims=True) for part in parts) * (1 / 2048)
            parts = [part - mean for part in parts]
            spread = sum(jnp.sum(part * part, axis=-1, keepdims=True) for part in parts)
            factor = lax.rsqrt(spread * (1 / 2048) + 1e-05)
            for n in range(4):
                lanes = slice(512 * n, 512 * n + 512)
                normed = (parts[n] * factor * merge_gain[:, lanes]).astype(BF)
                for c in range(2):
                    at = (c * 2 + g) * 144 + b * 48
                    merged[at : at + 48, lanes] = normed[48 * c : 48 * c + 48]
    loads[1].wait()
    for n in range(4):
        lanes = slice(256 * n, 256 * n + 256)
        coarse[:, lanes] = dot(merged[...], wm[:, lanes]).astype(BF)
    for w in range(4):
        at = slice(144 * w, 144 * w + 144)
        x_ref[at, :] = norm_block(coarse[at, :].astype(F32), gain_ref[...])
    loads[2].wait()
    for group in range(2):
        make_qkv(x_ref, wq, q_ref, k_ref, v_ref, tau_ref, sums_ref[...], 1024, group, 1024)
        attend(q_ref, k_ref, v_ref, mixed_ref, group * 512, None, masks_ref, tail_ref)
    loads[3].wait()
    for n in range(4):
        lanes = slice(256 * n, 256 * n + 256)
        update = dot(mixed_ref[...], wp[:, lanes])
        coarse[:, lanes] = (coarse[:, lanes].astype(F32) + update).astype(BF)
    loads[4].wait()
    for n in range(8):
        lanes = slice(256 * n, 256 * n + 256)
        split[:, lanes] = dot(coarse[...], ws[:, lanes]).astype(BF)
    for g in range(2):
        for b in range(3):
            parts = []
            for n in range(4):
                for c in range(2):
                    at = (c * 2 + g) * 144 + b * 48
                    parts.append(split[at : at + 48, 512 * n : 512 * n + 512])
            placed = dot(from_cells[...], jnp.concatenate(parts, axis=0))
            for side in range(2):
                here = grid.at[2 * g + side, pl.ds(192 * b, 192)]
                here[...] = (
                    here[...].astype(F32) + placed[192 * side : 192 * side + 192]
                ).astype(BF)
    store = pltpu.make_async_copy(grid, out_hbm, sem.at[0])
    store.start()
    store.wait()


def coarse_block(
    encoded, merge_gain, merge_weight, gain, w_qkv, w_proj, tau, w_split, tables, name
):
    return pl.pallas_call(
        coarse_kernel,
        out_shape=jax.ShapeDtypeStruct((4, 576, 512), BF),
        in_specs=[ANY, VMEM, ANY, VMEM, ANY, ANY, SMEM, ANY] + [VMEM] * 5,
        out_specs=ANY,
        scratch_shapes=[
            pltpu.VMEM((4, 576, 512), BF),
            pltpu.VMEM((2048, 1024), BF),
            pltpu.VMEM((1024, 3072), BF),
            pltpu.VMEM((1024, 1024), BF),
            pltpu.VMEM((1024, 2048), BF),
            pltpu.VMEM((576, 2048), BF),
            pltpu.VMEM((576, 1024), BF),
            pltpu.VMEM((576, 1024), BF),
            pltpu.VMEM((576, 512), BF),
            pltpu.VMEM((576, 512), BF),
            pltpu.VMEM((576, 512), BF),
            pltpu.VMEM((576, 1024), BF),
            pltpu.VMEM((576, 2048), BF),
            pltpu.SemaphoreType.DMA((5,)),
        ],
        compiler_params=pltpu.CompilerParams(vmem_limit_bytes=52 << 20),
        cost_estimate=pl.CostEstimate(
            flops=11_000_000_000, bytes_accessed=21_000_000, transcendentals=1_500_000
        ),
        name=name,
    )(
        encoded,
        merge_gain.reshape(1, 2048),
        merge_weight,
        gain.reshape(1, 1024),
        w_qkv,
        w_proj,
        tau,
        w_split,
        *tables,
    )


def local(
    tokens,
    enc_gain,
    enc_qkv,
    enc_proj,
    enc_tau,
    merge_gain,
    merge_weight,
    coarse_gain,
    coarse_qkv,
    coarse_proj,
    coarse_tau,
    expand_weight,
    dec_gain,
    dec_qkv,
    dec_proj,
    dec_tau,
):
    table = lambda values: jnp.asarray(values, BF)
    windows, cells = block_to_windows(), grid_to_cells()
    masks, tail, sums = table(half_masks()), table(tail_mask()), table(head_sums())
    fine_tables = (
        table(windows),
        table(windows.T),
        table(beside_to_block()),
        table(grid_to_beside()),
        jnp.asarray(differences()),
        masks,
        tail,
        sums,
    )
    coarse_tables = (table(cells), table(cells.T), masks, tail, sums)
    whole_qkv = lax.all_gather(coarse_qkv, "lon", axis=0, tiled=True)
    whole_proj = lax.all_gather(coarse_proj, "lon", axis=0, tiled=True)
    grid = tokens.reshape(4, 576, 512)
    encoded = fine_block(grid, enc_gain, enc_qkv, enc_proj, enc_tau, fine_tables, "encoder", 0)
    joined = coarse_block(
        encoded,
        merge_gain,
        merge_weight,
        coarse_gain,
        whole_qkv,
        whole_proj,
        coarse_tau,
        expand_weight,
        coarse_tables,
        "coarse",
    )
    decoded = fine_block(joined, dec_gain, dec_qkv, dec_proj, dec_tau, fine_tables, "decoder", 1)
    return decoded.reshape(4, 24, 24, 512)


def solution(mesh):
    placed = (
        P(None, "lat", "lon", None),
        P(),
        P(),
        P(),
        P(),
        P(),
        P(),
        P(),
        P("lon", None),
        P("lon", None),
        P(),
        P(),
        P(),
        P(),
        P(),
        P(),
    )
    return jax.shard_map(
        local, mesh=mesh, in_specs=placed, out_specs=P(None, "lat", "lon", None), check_vma=False
    )
```

```python
import functools

import jax
import jax.numpy as jnp
import numpy as np
from jax import lax
from jax.experimental import pallas as pl
from jax.experimental.pallas import tpu as pltpu
from jax.sharding import PartitionSpec as P

MESH = pl.DeviceIdType.MESH
BF = jnp.bfloat16
F32 = jnp.float32
LOG2E = 1.4426950408889634
NT = (((1,), (1,)), ((), ()))
HBM = pl.BlockSpec(memory_space=pltpu.HBM)
LEVELS = ((1, 2), (3, 0))


def dot(a, b):
    return jnp.dot(a, b, preferred_element_type=F32)


def beside_at(level, row, column):
    return (row // 2) * 16 + level * 6 + (row % 2) * 3 + column


def block_to_windows():
    table = np.zeros((192, 224), np.float32)
    for w in range(4):
        for level in range(2):
            for row in range(4):
                for c in range(6):
                    column = 3 + 6 * w + c
                    if column < 24:
                        source = level * 96 + row * 24 + column
                    else:
                        source = 192 + beside_at(level, row, column - 24)
                    table[w * 48 + level * 24 + row * 6 + c, source] = 1
    return table


def beside_to_block():
    table = np.zeros((192, 32), np.float32)
    for level in range(2):
        for row in range(4):
            for c in range(3):
                table[level * 96 + row * 24 + c, beside_at(level, row, c)] = 1
    return table


def block_row(block, row):
    if block < 4:
        return 6 + 4 * block + row
    if block == 4:
        return 22 + row if row < 2 else row - 2
    return 2 + row


def grid_to_beside():
    table = np.zeros((2, 192, 576), np.float32)
    for block in range(6):
        for level in range(2):
            for row in range(4):
                for c in range(3):
                    at = block * 32 + beside_at(level, row, c)
                    table[level, at, block_row(block, row) * 24 + c] = 1
    return table


def grid_to_cells():
    table = np.zeros((384, 384), np.float32)
    for pr in range(2):
        for pc in range(2):
            for cw in range(2):
                for level in range(2):
                    for i in range(4):
                        for j in range(6):
                            at = (pr * 2 + pc) * 96 + cw * 48 + level * 24 + i * 6 + j
                            source = level * 192 + (2 * i + pr) * 24 + 2 * (6 * cw + j) + pc
                            table[at, source] = 1
    return table


def differences():
    token = np.arange(144)
    level = (token // 24) % 2
    low = ((token // 48) * 4 + (token % 24) // 6) >= 6
    keys = np.concatenate([token[:128], np.tile(token[128:], 8)])
    by_level = (level[:, None] != level[keys][None]).astype(np.float32)
    by_row = (low[:, None] != low[keys][None]).astype(np.float32)
    return np.stack([by_level, by_row]) * np.float32(-1e30)


def half_masks():
    left = np.zeros((2, 128, 128), np.float32)
    left[0, :, :64] = 1
    left[1, :, 64:] = 1
    return left


def tail_mask():
    return (np.arange(128)[:, None] // 16 == np.arange(512)[None] // 64).astype(np.float32)


def head_sums():
    at = np.arange(256) // 64
    return (at[:, None] == at[None]).astype(np.float32)


def norm_block(values, gain):
    mean = jnp.mean(values, axis=-1, keepdims=True)
    center = values - mean
    spread = jnp.mean(center * center, axis=-1, keepdims=True)
    return (center * lax.rsqrt(spread + 1e-05) * gain).astype(BF)


def head_scale(tau_ref, first):
    at = lax.broadcasted_iota(jnp.int32, (1, 256), 1) // 64
    scale = jnp.zeros((1, 256), F32)
    for h in range(4):
        scale = jnp.where(at == h, tau_ref[:, first + h : first + h + 1], scale)
    return scale * LOG2E


def make_qkv(x_ref, w_ref, q_ref, k_ref, v_ref, tau_ref, sums, width, group):
    for half in range(2):
        at = group * 512 + half * 256
        lanes = slice(half * 256, half * 256 + 256)
        for part, target in ((0, q_ref), (1, k_ref)):
            product = dot(x_ref[...], w_ref[:, part * width + at : part * width + at + 256])
            rounded = product.astype(BF)
            total = dot(rounded * rounded, sums)
            factor = lax.rsqrt(total + 1e-06)
            if part == 0:
                factor = factor * head_scale(tau_ref, group * 8 + half * 4)
            target[:, lanes] = (product * factor).astype(BF)
        product = dot(x_ref[...], w_ref[:, 2 * width + at : 2 * width + at + 256])
        v_ref[:, lanes] = product.astype(BF)


def attend(q_ref, k_ref, v_ref, out_ref, out_at, bias_ref, masks_ref, tail_ref):
    def one_window(w, carry):
        row = pl.multiple_of(w * 144, 16)
        q = q_ref[pl.ds(row, 144), :]
        tail = tail_ref[...]
        left, right = masks_ref[0], masks_ref[1]
        k_tail = k_ref[pl.ds(pl.multiple_of(row + 128, 16), 16), :]
        v_tail = v_ref[pl.ds(pl.multiple_of(row + 128, 16), 16), :]
        k_tails = jnp.concatenate([k_tail] * 8, axis=0) * tail
        v_tails = jnp.concatenate([v_tail] * 8, axis=0) * tail
        score = lax.dot_general(q, k_tails, NT, preferred_element_type=F32)
        if bias_ref is not None:
            score = score + bias_ref[:, 128:]
        p_tail = jnp.exp2(score).astype(BF)
        for pair in range(4):
            lanes = slice(pair * 128, pair * 128 + 128)
            k = k_ref[pl.ds(row, 128), lanes]
            v = v_ref[pl.ds(row, 128), lanes]
            k_pair = jnp.concatenate([k * left, k * right], axis=0)
            score = lax.dot_general(q[:, lanes], k_pair, NT, preferred_element_type=F32)
            if bias_ref is not None:
                bias = bias_ref[:, :128]
                score = score + jnp.concatenate([bias, bias], axis=1)
            weight = jnp.exp2(score).astype(BF)
            v_pair = jnp.concatenate(
                [
                    jnp.concatenate([v * left, left], axis=1),
                    jnp.concatenate([v * right, right], axis=1),
                ],
                axis=0,
            )
            v_end = jnp.concatenate([v_tails[:, lanes], tail[:, lanes]], axis=1)
            both = dot(weight, v_pair) + dot(p_tail, v_end)
            mixed = (both[:, :128] / both[:, 128:]).astype(BF)
            out_ref[pl.ds(row, 144), pl.ds(out_at + pair * 128, 128)] = mixed
        return carry

    lax.fori_loop(0, 4, one_window, 0)


class Mover:
    def __init__(self, send_sem, recv_sem):
        self.send_sem, self.recv_sem = send_sem, recv_sem
        self.count = 0
        self.sent = []

    def send(self, source, target, device):
        copy = pltpu.make_async_remote_copy(
            src_ref=source,
            dst_ref=target,
            send_sem=self.send_sem.at[self.count],
            recv_sem=self.recv_sem.at[self.count],
            device_id=device,
            device_id_type=MESH,
        )
        copy.start()
        self.count += 1
        self.sent.append(copy)
        return copy

    def finish(self):
        for copy in self.sent:
            copy.wait_send()


class Place:
    def __init__(self, lat_size, lon_size):
        lat, lon = lax.axis_index("lat"), lax.axis_index("lon")
        self.lat, self.lon = lat, lon
        self.up, self.down = lax.rem(lat + lat_size - 1, lat_size), lax.rem(lat + 1, lat_size)
        self.west, self.east = lax.rem(lon + lon_size - 1, lon_size), lax.rem(lon + 1, lon_size)
        self.last = (lat == lat_size - 1).astype(F32)
        self.x_next, self.x_last = lax.rem(lon + 4, 16), lax.rem(lon + 12, 16)
        self.x_far = lax.rem(lon + 8, 16)
        self.mate = lon + 1 - 2 * lax.rem(lon, 2)
        self.across = lon + 2 - 4 * lax.rem(lon // 2, 2)
        self.z = lat // 2
        self.other_z = tuple(lax.rem(lat + 2 * n, 8) for n in (1, 3, 2))
        self.halo = (
            (self.up, lon),
            (self.down, lon),
            (lat, self.west),
            (lat, self.east),
            (self.up, self.west),
            (self.down, self.east),
        )
        self.gather = (
            (lat, self.x_next),
            (lat, self.x_last),
            (lat, self.mate),
            (lat, self.across),
        ) + tuple((other, lon) for other in self.other_z)


class Gather:
    def __init__(self, place, rows, mover):
        self.place, self.rows, self.mover = place, rows, mover
        self.from_mate = []

    def part(self, owner, first, size):
        return self.rows.at[pl.ds(pl.multiple_of(owner * 64 + first, 16), size)]

    def send(self, owner, first, size, device):
        part = self.part(owner, first, size)
        return self.mover.send(part, part, device)

    def to_mate(self, owner):
        place = self.place
        self.from_mate.append(self.send(owner, 0, 64, (place.lat, place.mate)))

    def along_x(self, owner):
        place = self.place
        return (
            self.send(owner, 0, 64, (place.lat, place.x_next)),
            self.send(owner, 0, 64, (place.lat, place.x_last)),
        )

    def relay_x(self, before, after):
        place = self.place
        return (
            self.send(before, 0, 32, (place.lat, place.x_next)),
            self.send(after, 32, 32, (place.lat, place.x_last)),
        )

    def start(self):
        place = self.place
        self.near = self.along_x(place.lon)
        quarter = pl.multiple_of(place.z * 16, 16)
        self.quarter = self.send(place.lon, quarter, 16, (place.lat, place.across))
        self.to_mate(place.lon)

    def second(self):
        place = self.place
        for copy in self.near:
            copy.wait_recv()
        self.far = self.relay_x(place.x_last, place.x_next)
        self.quarter.wait_recv()
        quarter = pl.multiple_of(place.z * 16, 16)
        self.quarters = [
            self.send(place.across, quarter, 16, (other, place.lon)) for other in place.other_z
        ]
        self.to_mate(place.x_last)
        self.to_mate(place.x_next)

    def across_of(self, lon):
        return lon + 2 - 4 * lax.rem(lon // 2, 2)

    def third(self):
        place = self.place
        for copy in self.quarters:
            copy.wait_recv()
        self.near = self.along_x(place.across)
        for copy in self.far:
            copy.wait_recv()
        self.to_mate(place.x_far)
        self.to_mate(place.across)

    def fourth(self):
        place = self.place
        for copy in self.near:
            copy.wait_recv()
        before, after = self.across_of(place.x_last), self.across_of(place.x_next)
        self.far = self.relay_x(before, after)
        self.to_mate(before)
        self.to_mate(after)

    def fifth(self):
        for copy in self.far:
            copy.wait_recv()
        self.to_mate(self.across_of(self.place.x_far))

    def finish(self):
        for copy in self.from_mate:
            copy.wait_recv()


def fine_block(grid, gain, wq, wp, tau, place, tables, work, comm, copy_sem, between):
    to_windows, from_windows, spread_ref, pick_ref, diff_ref, masks_ref, tail_ref, sums_ref = tables
    x_ref, q_ref, k_ref, v_ref, mixed_ref, shifted_ref, bias_ref = work
    blocks, picked, row_out, col_out, row_in, col_in, there_sems, back_sems = comm
    there, back = Mover(*there_sems), Mover(*back_sems)
    lat, lon = place.lat, place.lon
    rows, columns, backs = {}, {}, {}

    def send_rows(g):
        for side in range(2):
            level = LEVELS[g][side]
            rows[g, side, 0] = there.send(
                grid.at[level, pl.ds(0, 48)],
                blocks.at[g, 4, pl.ds(96 * side + 48, 48)],
                (place.up, lon),
            )
            rows[g, side, 1] = there.send(
                grid.at[level, pl.ds(48, 96)],
                blocks.at[g, 5, pl.ds(96 * side, 96)],
                (place.up, lon),
            )

    def send_columns(g):
        picks = dot(pick_ref[0], grid[LEVELS[g][0]]) + dot(pick_ref[1], grid[LEVELS[g][1]])
        for b in range(6):
            picked[g, b] = picks[32 * b : 32 * b + 32].astype(BF)
        columns[g, 0] = there.send(
            picked.at[g, pl.ds(0, 4)], blocks.at[g, pl.ds(0, 4), pl.ds(192, 32)], (lat, place.west)
        )
        columns[g, 1] = there.send(
            picked.at[g, 4, pl.ds(0, 16)], blocks.at[g, 4, pl.ds(192, 16)], (lat, place.west)
        )
        columns[g, 2] = there.send(
            picked.at[g, 4, pl.ds(16, 16)], blocks.at[g, 4, pl.ds(208, 16)], (place.up, place.west)
        )
        columns[g, 3] = there.send(
            picked.at[g, 5], blocks.at[g, 5, pl.ds(192, 32)], (place.up, place.west)
        )

    send_rows(0)
    own = []
    for g in range(2):
        for side in range(2):
            level = LEVELS[g][side]
            for b in range(5):
                size = 96 if b < 4 else 48
                copy = pltpu.make_async_copy(
                    grid.at[level, pl.ds(144 + 96 * b, size)],
                    blocks.at[g, b, pl.ds(96 * side, size)],
                    copy_sem.at[(g * 2 + side) * 5 + b],
                )
                copy.start()
                own.append(copy)
    send_columns(0)
    send_columns(1)
    for copy in own:
        copy.wait()

    def add_rows(level, at, size, values):
        grid[level, pl.ds(at, size), :] = (
            grid[level, pl.ds(at, size), :].astype(F32) + values
        ).astype(BF)

    for g in range(2):
        for half in range(2):
            if half == 0:
                columns[g, 0].wait_recv()
            else:
                for part in (1, 2, 3):
                    columns[g, part].wait_recv()
                for side in range(2):
                    rows[g, side, 0].wait_recv()
                    rows[g, side, 1].wait_recv()
            for b in range(3):
                tokens_in = dot(to_windows[...], blocks[g, 3 * half + b])
                normed = norm_block(tokens_in, gain[...])
                for w in range(4):
                    x_ref[w * 144 + b * 48 : w * 144 + b * 48 + 48, :] = normed[
                        48 * w : 48 * w + 48
                    ]
            make_qkv(x_ref, wq, q_ref, k_ref, v_ref, tau, sums_ref[...], 512, 0)
            masked = g == 1 or half == 1
            if masked:
                bias = jnp.zeros((144, 256), F32)
                if g == 1:
                    bias = bias + diff_ref[0]
                if half == 1:
                    bias = bias + diff_ref[1] * place.last
                bias_ref[...] = bias
            attend(
                q_ref, k_ref, v_ref, mixed_ref, 0, bias_ref if masked else None, masks_ref, tail_ref
            )
            shifted_ref[...] = dot(mixed_ref[...], wp[...]).astype(BF)
            for b in range(3):
                index = 3 * half + b
                parts = [
                    shifted_ref[w * 144 + b * 48 : w * 144 + b * 48 + 48, :] for w in range(4)
                ]
                placed = dot(from_windows[...], jnp.concatenate(parts, axis=0))
                col_out[g, index] = placed[192:224].astype(BF)
                for side in range(2):
                    level = LEVELS[g][side]
                    mine = placed[96 * side : 96 * side + 96]
                    if index < 4:
                        add_rows(level, 144 + 96 * index, 96, mine)
                    elif index == 4:
                        add_rows(level, 528, 48, mine[:48])
                        row_out[g, 48 * side : 48 * side + 48, :] = mine[48:].astype(BF)
                    else:
                        row_out[g, 96 + 96 * side : 192 + 96 * side, :] = mine.astype(BF)
            if half == 1:
                backs[g, 0] = back.send(row_out.at[g], row_in.at[g], (place.down, lon))
                backs[g, 1] = back.send(
                    col_out.at[g, pl.ds(0, 4)], col_in.at[g, pl.ds(0, 4)], (lat, place.east)
                )
                backs[g, 2] = back.send(
                    col_out.at[g, 4, pl.ds(0, 16)],
                    col_in.at[g, 4, pl.ds(0, 16)],
                    (lat, place.east),
                )
                backs[g, 3] = back.send(
                    col_out.at[g, 4, pl.ds(16, 16)],
                    col_in.at[g, 4, pl.ds(16, 16)],
                    (place.down, place.east),
                )
                backs[g, 4] = back.send(col_out.at[g, 5], col_in.at[g, 5], (place.down, place.east))
            if g == 0 and half == 0:
                send_rows(1)
            between[2 * g + half]()

    there.finish()
    for g in range(2):
        for part in range(1, 5):
            backs[g, part].wait_recv()
        for b in range(4):
            placed = dot(spread_ref[...], col_in[g, b])
            for side in range(2):
                add_rows(LEVELS[g][side], 144 + 96 * b, 96, placed[96 * side : 96 * side + 96])
        backs[g, 0].wait_recv()
        placed = dot(spread_ref[...], col_in[g, 4])
        for side in range(2):
            mine = placed[96 * side : 96 * side + 96]
            add_rows(LEVELS[g][side], 528, 48, mine[:48])
            above = row_in[g, 48 * side : 48 * side + 48, :].astype(F32)
            add_rows(LEVELS[g][side], 0, 48, mine[48:] + above)
        placed = dot(spread_ref[...], col_in[g, 5])
        for side in range(2):
            above = row_in[g, 96 + 96 * side : 192 + 96 * side, :].astype(F32)
            add_rows(LEVELS[g][side], 48, 96, placed[96 * side : 96 * side + 96] + above)
    back.finish()


def coarse_block(grid, gains, weights, tau, tables, work, loaded, gather):
    merge_gain, gain = gains
    wm, wc, ws = weights
    to_cells, from_cells, masks_ref, tail_ref, sums_ref = tables
    merged, coarse, x_ref, q_ref, k_ref, v_ref, mixed_ref, split = work
    for g in range(2):
        for b in range(3):
            cells = dot(to_cells[:, :192], grid[2 * g, pl.ds(192 * b, 192), :]) + dot(
                to_cells[:, 192:], grid[2 * g + 1, pl.ds(192 * b, 192), :]
            )
            parts = [cells[96 * n : 96 * n + 96] for n in range(4)]
            mean = sum(jnp.sum(part, axis=-1, keepdims=True) for part in parts) * (1 / 2048)
            parts = [part - mean for part in parts]
            spread = sum(jnp.sum(part * part, axis=-1, keepdims=True) for part in parts)
            factor = lax.rsqrt(spread * (1 / 2048) + 1e-05)
            for n in range(4):
                lanes = slice(512 * n, 512 * n + 512)
                normed = (parts[n] * factor * merge_gain[:, lanes]).astype(BF)
                for c in range(2):
                    at = (c * 2 + g) * 144 + b * 48
                    merged[at : at + 48, lanes] = normed[48 * c : 48 * c + 48]
    loaded[0].wait()
    for n in range(4):
        lanes = slice(256 * n, 256 * n + 256)
        coarse[:, lanes] = dot(merged[...], wm[:, lanes]).astype(BF)
        if n == 0:
            gather.fifth()
    for w in range(4):
        at = slice(144 * w, 144 * w + 144)
        x_ref[at, :] = norm_block(coarse[at, :].astype(F32), gain[...])
    gather.finish()
    for group in range(2):
        make_qkv(x_ref, wc, q_ref, k_ref, v_ref, tau, sums_ref[...], 1024, group)
        attend(q_ref, k_ref, v_ref, mixed_ref, group * 512, None, masks_ref, tail_ref)
    for n in range(4):
        lanes = slice(256 * n, 256 * n + 256)
        update = dot(mixed_ref[...], wc[:, 3072 + 256 * n : 3328 + 256 * n])
        coarse[:, lanes] = (coarse[:, lanes].astype(F32) + update).astype(BF)
    loaded[1].wait()
    for n in range(8):
        lanes = slice(256 * n, 256 * n + 256)
        split[:, lanes] = dot(coarse[...], ws[:, lanes]).astype(BF)
    for g in range(2):
        for b in range(3):
            parts = []
            for n in range(4):
                for c in range(2):
                    at = (c * 2 + g) * 144 + b * 48
                    parts.append(split[at : at + 48, 512 * n : 512 * n + 512])
            placed = dot(from_cells[...], jnp.concatenate(parts, axis=0))
            for side in range(2):
                here = grid.at[2 * g + side, pl.ds(192 * b, 192)]
                here[...] = (
                    here[...].astype(F32) + placed[192 * side : 192 * side + 192]
                ).astype(BF)


SCRATCH = {
    "grid": ((4, 576, 512), BF),
    "blocks": ((2, 6, 224, 512), BF),
    "picked": ((2, 6, 32, 512), BF),
    "row_out": ((2, 288, 512), BF),
    "col_out": ((2, 6, 32, 512), BF),
    "row_in": ((2, 288, 512), BF),
    "col_in": ((2, 6, 32, 512), BF),
    "x_fine": ((576, 512), BF),
    "q": ((576, 512), BF),
    "k": ((576, 512), BF),
    "v": ((576, 512), BF),
    "mixed_fine": ((576, 512), BF),
    "shifted": ((576, 512), BF),
    "bias": ((144, 256), F32),
    "merged": ((576, 2048), BF),
    "coarse": ((576, 1024), BF),
    "x_coarse": ((576, 1024), BF),
    "mixed_coarse": ((576, 1024), BF),
    "split": ((576, 2048), BF),
    "coarse_weights": ((1024, 4096), BF),
}
SEMAPHORES = {
    "load": 40,
    "copy": 20,
    "there_send": 16,
    "there_recv": 16,
    "back_send": 10,
    "back_recv": 10,
    "gather_send": 20,
    "gather_recv": 20,
}


def kernel(lat_size, lon_size, names, *refs):
    count = len(names)
    given = dict(zip(names, refs[:count]))
    out = refs[count]
    held = dict(zip(names[3:], refs[count + 1 :]))
    rest = refs[count + 1 + count - 3 :]
    at = dict(zip(list(SCRATCH) + list(SEMAPHORES), rest))
    place = Place(lat_size, lon_size)
    grid, whole = at["grid"], at["coarse_weights"]
    start = pl.ds(pl.multiple_of(place.lon * 64, 16), 64)
    loads = {}

    def load(name, source, target):
        loads[name] = pltpu.make_async_copy(source, target, at["load"].at[len(loads)])
        loads[name].start()

    load("tokens", given["tokens"], grid)
    load("coarse_qkv", given["coarse_qkv"], whole.at[start, pl.ds(0, 3072)])
    load("coarse_proj", given["coarse_proj"], whole.at[start, pl.ds(3072, 1024)])
    for name in names[3:]:
        load(name, given[name], held[name])

    barrier = pltpu.get_barrier_semaphore()
    partners = place.halo + place.gather
    for device in partners:
        pl.semaphore_signal(barrier, inc=1, device_id=device, device_id_type=MESH)
    pl.semaphore_wait(barrier, len(partners))

    gather = Gather(place, whole, Mover(at["gather_send"], at["gather_recv"]))
    loads["coarse_qkv"].wait()
    loads["coarse_proj"].wait()
    loads["tokens"].wait()
    gather.start()
    late = ("merge_weight", "expand_weight")
    for name in names[3:]:
        if name not in late:
            loads[name].wait()

    fine_tables = [
        held[name]
        for name in ("windows", "windows_t", "spread", "pick", "differ", "masks", "tail", "sums")
    ]
    work = [at[name] for name in ("x_fine", "q", "k", "v", "mixed_fine", "shifted", "bias")]
    comm = [at[name] for name in ("blocks", "picked", "row_out", "col_out", "row_in", "col_in")]
    comm += [(at["there_send"], at["there_recv"]), (at["back_send"], at["back_recv"])]
    nothing = lambda: None

    def fine(prefix, between):
        fine_block(
            grid,
            held[prefix + "_gain"],
            held[prefix + "_qkv"],
            held[prefix + "_proj"],
            held[prefix + "_tau"],
            place,
            fine_tables,
            work,
            comm,
            at["copy"],
            between,
        )

    fine("enc", (gather.second, gather.third, nothing, gather.fourth))
    coarse_block(
        grid,
        (held["merge_gain"], held["coarse_gain"]),
        (held["merge_weight"], whole, held["expand_weight"]),
        held["coarse_tau"],
        [held[name] for name in ("cells", "cells_t", "masks", "tail", "sums")],
        [
            at[name]
            for name in (
                "merged",
                "coarse",
                "x_coarse",
                "q",
                "k",
                "v",
                "mixed_coarse",
                "split",
            )
        ],
        [loads[name] for name in late],
        gather,
    )
    gather.mover.finish()
    fine("dec", (nothing,) * 4)
    store = pltpu.make_async_copy(grid, out, at["load"].at[0])
    store.start()
    store.wait()


def local(
    tokens,
    enc_gain,
    enc_qkv,
    enc_proj,
    enc_tau,
    merge_gain,
    merge_weight,
    coarse_gain,
    coarse_qkv,
    coarse_proj,
    coarse_tau,
    expand_weight,
    dec_gain,
    dec_qkv,
    dec_proj,
    dec_tau,
):
    table = lambda values: jnp.asarray(values, BF)
    row = lambda values: values.reshape(1, -1)
    windows, cells = block_to_windows(), grid_to_cells()
    given = {
        "tokens": tokens.reshape(4, 576, 512),
        "coarse_qkv": coarse_qkv,
        "coarse_proj": coarse_proj,
        "enc_gain": row(enc_gain),
        "enc_tau": row(enc_tau),
        "pick": table(grid_to_beside()),
        "windows": table(windows),
        "enc_qkv": enc_qkv,
        "sums": table(head_sums()),
        "masks": table(half_masks()),
        "tail": table(tail_mask()),
        "enc_proj": enc_proj,
        "windows_t": table(windows.T),
        "spread": table(beside_to_block()),
        "differ": jnp.asarray(differences()),
        "merge_gain": row(merge_gain),
        "coarse_gain": row(coarse_gain),
        "coarse_tau": row(coarse_tau),
        "dec_gain": row(dec_gain),
        "dec_tau": row(dec_tau),
        "dec_qkv": dec_qkv,
        "dec_proj": dec_proj,
        "cells": table(cells),
        "cells_t": table(cells.T),
        "merge_weight": merge_weight,
        "expand_weight": expand_weight,
    }
    names = tuple(given)
    scratch = [pltpu.VMEM(given[name].shape, given[name].dtype) for name in names[3:]]
    scratch += [pltpu.VMEM(shape, dtype) for shape, dtype in SCRATCH.values()]
    scratch += [pltpu.SemaphoreType.DMA((n,)) for n in SEMAPHORES.values()]
    decoded = pl.pallas_call(
        functools.partial(kernel, lax.axis_size("lat"), lax.axis_size("lon"), names),
        out_shape=jax.ShapeDtypeStruct((4, 576, 512), BF),
        in_specs=[HBM] * len(names),
        out_specs=HBM,
        scratch_shapes=scratch,
        compiler_params=pltpu.CompilerParams(
            collective_id=0, has_side_effects=True, vmem_limit_bytes=60 << 20
        ),
        cost_estimate=pl.CostEstimate(
            flops=35_000_000_000, bytes_accessed=30_000_000, transcendentals=8_000_000
        ),
        name="blocks",
    )(*given.values())
    return decoded.reshape(4, 24, 24, 512)


def solution(mesh):
    placed = (
        P(None, "lat", "lon", None),
        P(),
        P(),
        P(),
        P(),
        P(),
        P(),
        P(),
        P("lon", None),
        P("lon", None),
        P(),
        P(),
        P(),
        P(),
        P(),
        P(),
    )
    return jax.shard_map(
        local, mesh=mesh, in_specs=placed, out_specs=P(None, "lat", "lon", None), check_vma=False
    )
```

```python
import functools

import jax
import jax.numpy as jnp
import numpy as np
from jax import lax
from jax.experimental import pallas as pl
from jax.experimental.pallas import tpu as pltpu
from jax.sharding import PartitionSpec as P

MESH = pl.DeviceIdType.MESH
BF = jnp.bfloat16
F32 = jnp.float32
LOG2E = 1.4426950408889634
NT = (((1,), (1,)), ((), ()))
HBM = pl.BlockSpec(memory_space=pltpu.HBM)
LEVELS = ((1, 2), (3, 0))


def dot(a, b):
    return jnp.dot(a, b, preferred_element_type=F32)


def beside_at(level, row, column):
    return (row // 2) * 16 + level * 6 + (row % 2) * 3 + column


def block_to_windows():
    table = np.zeros((192, 224), np.float32)
    for w in range(4):
        for level in range(2):
            for row in range(4):
                for c in range(6):
                    column = 3 + 6 * w + c
                    if column < 24:
                        source = level * 96 + row * 24 + column
                    else:
                        source = 192 + beside_at(level, row, column - 24)
                    table[w * 48 + level * 24 + row * 6 + c, source] = 1
    return table


def beside_to_block():
    table = np.zeros((192, 32), np.float32)
    for level in range(2):
        for row in range(4):
            for c in range(3):
                table[level * 96 + row * 24 + c, beside_at(level, row, c)] = 1
    return table


def block_row(block, row):
    if block < 4:
        return 6 + 4 * block + row
    if block == 4:
        return 22 + row if row < 2 else row - 2
    return 2 + row


def grid_to_beside():
    table = np.zeros((2, 192, 576), np.float32)
    for block in range(6):
        for level in range(2):
            for row in range(4):
                for c in range(3):
                    at = block * 32 + beside_at(level, row, c)
                    table[level, at, block_row(block, row) * 24 + c] = 1
    return table


def grid_to_cells():
    table = np.zeros((384, 384), np.float32)
    for pr in range(2):
        for pc in range(2):
            for cw in range(2):
                for level in range(2):
                    for i in range(4):
                        for j in range(6):
                            at = (pr * 2 + pc) * 96 + cw * 48 + level * 24 + i * 6 + j
                            source = level * 192 + (2 * i + pr) * 24 + 2 * (6 * cw + j) + pc
                            table[at, source] = 1
    return table


def differences():
    token = np.arange(144)
    level = (token // 24) % 2
    low = ((token // 48) * 4 + (token % 24) // 6) >= 6
    keys = np.concatenate([token[:128], np.tile(token[128:], 8)])
    by_level = (level[:, None] != level[keys][None]).astype(np.float32)
    by_row = (low[:, None] != low[keys][None]).astype(np.float32)
    return np.stack([by_level, by_row]) * np.float32(-1e30)


def half_masks():
    left = np.zeros((2, 128, 128), np.float32)
    left[0, :, :64] = 1
    left[1, :, 64:] = 1
    return left


def tail_mask():
    return (np.arange(128)[:, None] // 16 == np.arange(512)[None] // 64).astype(np.float32)


def head_sums():
    at = np.arange(256) // 64
    return (at[:, None] == at[None]).astype(np.float32)


def norm_block(values, gain):
    mean = jnp.mean(values, axis=-1, keepdims=True)
    center = values - mean
    spread = jnp.mean(center * center, axis=-1, keepdims=True)
    return (center * lax.rsqrt(spread + 1e-05) * gain).astype(BF)


def head_scale(tau_ref, first):
    at = lax.broadcasted_iota(jnp.int32, (1, 256), 1) // 64
    scale = jnp.zeros((1, 256), F32)
    for h in range(4):
        scale = jnp.where(at == h, tau_ref[:, first + h : first + h + 1], scale)
    return scale * LOG2E


def make_qkv(x_ref, w_ref, q_ref, k_ref, v_ref, tau_ref, sums, width, group):
    def product(target, part, half):
        at = part * width + group * 512 + half * 256
        target[:, half * 256 : half * 256 + 256] = dot(x_ref[...], w_ref[:, at : at + 256]).astype(BF)

    def unit(target, half, scaled):
        lanes = slice(half * 256, half * 256 + 256)
        values = target[:, lanes]
        factor = lax.rsqrt(dot(values * values, sums) + 1e-06)
        if scaled:
            factor = factor * head_scale(tau_ref, group * 8 + half * 4)
        target[:, lanes] = (values.astype(F32) * factor).astype(BF)

    product(q_ref, 0, 0)
    product(q_ref, 0, 1)
    unit(q_ref, 0, True)
    product(k_ref, 1, 0)
    unit(q_ref, 1, True)
    product(k_ref, 1, 1)
    unit(k_ref, 0, False)
    product(v_ref, 2, 0)
    unit(k_ref, 1, False)
    product(v_ref, 2, 1)


def attend(q_ref, k_ref, v_ref, out_ref, out_at, bias_ref, masks_ref, tail_ref, weight_ref):
    left, right = masks_ref[0], masks_ref[1]
    tail = tail_ref[...]

    def weights(score, bias):
        return jnp.exp2(score if bias is None else score + bias).astype(BF)

    bias_main = bias_tail = None
    if bias_ref is not None:
        bias_main = jnp.concatenate([bias_ref[:, :128], bias_ref[:, :128]], axis=1)
        bias_tail = bias_ref[:, 128:]
    for w in range(4):
        row = w * 144
        rows = slice(row, row + 144)
        q = q_ref[rows, :]
        k_tails = jnp.concatenate([k_ref[row + 128 : row + 144, :]] * 8, axis=0) * tail
        score = lax.dot_general(q, k_tails, NT, preferred_element_type=F32)
        weight_tail = weights(score, bias_tail)
        for pair in range(4):
            lanes = slice(pair * 128, pair * 128 + 128)
            k = k_ref[row : row + 128, lanes]
            k_pair = jnp.concatenate([k * left, k * right], axis=0)
            score = lax.dot_general(q[:, lanes], k_pair, NT, preferred_element_type=F32)
            weight_ref[rows, pair * 384 : pair * 384 + 256] = weights(score, bias_main)
            weight_ref[rows, pair * 384 + 256 : pair * 384 + 384] = weight_tail
    for w in range(4):
        row = w * 144
        rows = slice(row, row + 144)
        v_tails = jnp.concatenate([v_ref[row + 128 : row + 144, :]] * 8, axis=0) * tail
        for pair in range(4):
            lanes = slice(pair * 128, pair * 128 + 128)
            v = v_ref[row : row + 128, lanes]
            v_pair = jnp.concatenate(
                [
                    jnp.concatenate([v * left, left], axis=1),
                    jnp.concatenate([v * right, right], axis=1),
                    jnp.concatenate([v_tails[:, lanes], tail[:, lanes]], axis=1),
                ],
                axis=0,
            )
            both = dot(weight_ref[rows, pair * 384 : pair * 384 + 384], v_pair)
            mixed = (both[:, :128] / both[:, 128:]).astype(BF)
            out_ref[rows, out_at + pair * 128 : out_at + pair * 128 + 128] = mixed


class Mover:
    def __init__(self, send_sem, recv_sem):
        self.send_sem, self.recv_sem = send_sem, recv_sem
        self.count = 0
        self.sent = []

    def send(self, source, target, device):
        copy = pltpu.make_async_remote_copy(
            src_ref=source,
            dst_ref=target,
            send_sem=self.send_sem.at[self.count],
            recv_sem=self.recv_sem.at[self.count],
            device_id=device,
            device_id_type=MESH,
        )
        copy.start()
        self.count += 1
        self.sent.append(copy)
        return copy

    def finish(self):
        for copy in self.sent:
            copy.wait_send()


class Place:
    def __init__(self, lat_size, lon_size):
        lat, lon = lax.axis_index("lat"), lax.axis_index("lon")
        self.lat, self.lon = lat, lon
        self.up, self.down = lax.rem(lat + lat_size - 1, lat_size), lax.rem(lat + 1, lat_size)
        self.west, self.east = lax.rem(lon + lon_size - 1, lon_size), lax.rem(lon + 1, lon_size)
        self.last = (lat == lat_size - 1).astype(F32)
        self.x_next, self.x_last = lax.rem(lon + 4, 16), lax.rem(lon + 12, 16)
        self.x_far = lax.rem(lon + 8, 16)
        self.mate = lon + 1 - 2 * lax.rem(lon, 2)
        self.across = lon + 2 - 4 * lax.rem(lon // 2, 2)
        self.z = lat // 2
        self.other_z = tuple(lax.rem(lat + 2 * n, 8) for n in (1, 3, 2))
        self.halo = (
            (self.up, lon),
            (self.down, lon),
            (lat, self.west),
            (lat, self.east),
            (self.up, self.west),
            (self.down, self.east),
        )
        self.gather = (
            (lat, self.x_next),
            (lat, self.x_last),
            (lat, self.mate),
            (lat, self.across),
        ) + tuple((other, lon) for other in self.other_z)


class Gather:
    def __init__(self, place, rows, mover):
        self.place, self.rows, self.mover = place, rows, mover
        self.from_mate = []

    def part(self, owner, first, size):
        return self.rows.at[pl.ds(pl.multiple_of(owner * 64 + first, 16), size)]

    def send(self, owner, first, size, device):
        part = self.part(owner, first, size)
        return self.mover.send(part, part, device)

    def to_mate(self, owner):
        place = self.place
        self.from_mate.append(self.send(owner, 0, 64, (place.lat, place.mate)))

    def along_x(self, owner):
        place = self.place
        return (
            self.send(owner, 0, 64, (place.lat, place.x_next)),
            self.send(owner, 0, 64, (place.lat, place.x_last)),
        )

    def relay_x(self, before, after):
        place = self.place
        return (
            self.send(before, 0, 32, (place.lat, place.x_next)),
            self.send(after, 32, 32, (place.lat, place.x_last)),
        )

    def start(self):
        place = self.place
        self.near = self.along_x(place.lon)
        quarter = pl.multiple_of(place.z * 16, 16)
        self.quarter = self.send(place.lon, quarter, 16, (place.lat, place.across))
        self.to_mate(place.lon)

    def second(self):
        place = self.place
        for copy in self.near:
            copy.wait_recv()
        self.far = self.relay_x(place.x_last, place.x_next)
        self.quarter.wait_recv()
        quarter = pl.multiple_of(place.z * 16, 16)
        self.quarters = [
            self.send(place.across, quarter, 16, (other, place.lon)) for other in place.other_z
        ]
        self.to_mate(place.x_last)
        self.to_mate(place.x_next)

    def across_of(self, lon):
        return lon + 2 - 4 * lax.rem(lon // 2, 2)

    def third(self):
        place = self.place
        for copy in self.quarters:
            copy.wait_recv()
        self.near = self.along_x(place.across)
        for copy in self.far:
            copy.wait_recv()
        self.to_mate(place.x_far)
        self.to_mate(place.across)

    def fourth(self):
        place = self.place
        for copy in self.near:
            copy.wait_recv()
        before, after = self.across_of(place.x_last), self.across_of(place.x_next)
        self.far = self.relay_x(before, after)
        self.to_mate(before)
        self.to_mate(after)

    def fifth(self):
        for copy in self.far:
            copy.wait_recv()
        self.to_mate(self.across_of(self.place.x_far))

    def finish(self):
        for copy in self.from_mate:
            copy.wait_recv()


def fine_block(grid, gain, wq, wp, tau, place, tables, work, comm, copy_sem, between):
    to_windows, from_windows, spread_ref, pick_ref, diff_ref, masks_ref, tail_ref, sums_ref = tables
    x_ref, q_ref, k_ref, v_ref, mixed_ref, shifted_ref, bias_ref, weight_ref = work
    blocks, picked, row_out, col_out, row_in, col_in, there_sems, back_sems = comm
    there, back = Mover(*there_sems), Mover(*back_sems)
    lat, lon = place.lat, place.lon
    rows, columns, backs = {}, {}, {}

    def send_rows(g):
        for side in range(2):
            level = LEVELS[g][side]
            rows[g, side, 0] = there.send(
                grid.at[level, pl.ds(0, 48)],
                blocks.at[g, 4, pl.ds(96 * side + 48, 48)],
                (place.up, lon),
            )
            rows[g, side, 1] = there.send(
                grid.at[level, pl.ds(48, 96)],
                blocks.at[g, 5, pl.ds(96 * side, 96)],
                (place.up, lon),
            )

    def send_columns(g):
        picks = dot(pick_ref[0], grid[LEVELS[g][0]]) + dot(pick_ref[1], grid[LEVELS[g][1]])
        for b in range(6):
            picked[g, b] = picks[32 * b : 32 * b + 32].astype(BF)
        columns[g, 0] = there.send(
            picked.at[g, pl.ds(0, 4)], blocks.at[g, pl.ds(0, 4), pl.ds(192, 32)], (lat, place.west)
        )
        columns[g, 1] = there.send(
            picked.at[g, 4, pl.ds(0, 16)], blocks.at[g, 4, pl.ds(192, 16)], (lat, place.west)
        )
        columns[g, 2] = there.send(
            picked.at[g, 4, pl.ds(16, 16)], blocks.at[g, 4, pl.ds(208, 16)], (place.up, place.west)
        )
        columns[g, 3] = there.send(
            picked.at[g, 5], blocks.at[g, 5, pl.ds(192, 32)], (place.up, place.west)
        )

    send_rows(0)
    own = []
    for g in range(2):
        for side in range(2):
            level = LEVELS[g][side]
            for b in range(5):
                size = 96 if b < 4 else 48
                copy = pltpu.make_async_copy(
                    grid.at[level, pl.ds(144 + 96 * b, size)],
                    blocks.at[g, b, pl.ds(96 * side, size)],
                    copy_sem.at[(g * 2 + side) * 5 + b],
                )
                copy.start()
                own.append(copy)
    send_columns(0)
    send_columns(1)
    for copy in own:
        copy.wait()

    def add_rows(level, at, size, values):
        grid[level, pl.ds(at, size), :] = (
            grid[level, pl.ds(at, size), :].astype(F32) + values
        ).astype(BF)

    for g in range(2):
        for half in range(2):
            if half == 0:
                columns[g, 0].wait_recv()
            else:
                for part in (1, 2, 3):
                    columns[g, part].wait_recv()
                for side in range(2):
                    rows[g, side, 0].wait_recv()
                    rows[g, side, 1].wait_recv()
            for b in range(3):
                tokens_in = dot(to_windows[...], blocks[g, 3 * half + b])
                normed = norm_block(tokens_in, gain[...])
                for w in range(4):
                    x_ref[w * 144 + b * 48 : w * 144 + b * 48 + 48, :] = normed[
                        48 * w : 48 * w + 48
                    ]
            make_qkv(x_ref, wq, q_ref, k_ref, v_ref, tau, sums_ref[...], 512, 0)
            masked = g == 1 or half == 1
            if masked:
                bias = jnp.zeros((144, 256), F32)
                if g == 1:
                    bias = bias + diff_ref[0]
                if half == 1:
                    bias = bias + diff_ref[1] * place.last
                bias_ref[...] = bias
            attend(
                q_ref,
                k_ref,
                v_ref,
                mixed_ref,
                0,
                bias_ref if masked else None,
                masks_ref,
                tail_ref,
                weight_ref,
            )
            shifted_ref[...] = dot(mixed_ref[...], wp[...]).astype(BF)
            for b in range(3):
                index = 3 * half + b
                parts = [
                    shifted_ref[w * 144 + b * 48 : w * 144 + b * 48 + 48, :] for w in range(4)
                ]
                placed = dot(from_windows[...], jnp.concatenate(parts, axis=0))
                col_out[g, index] = placed[192:224].astype(BF)
                for side in range(2):
                    level = LEVELS[g][side]
                    mine = placed[96 * side : 96 * side + 96]
                    if index < 4:
                        add_rows(level, 144 + 96 * index, 96, mine)
                    elif index == 4:
                        add_rows(level, 528, 48, mine[:48])
                        row_out[g, 48 * side : 48 * side + 48, :] = mine[48:].astype(BF)
                    else:
                        row_out[g, 96 + 96 * side : 192 + 96 * side, :] = mine.astype(BF)
            if half == 1:
                backs[g, 0] = back.send(row_out.at[g], row_in.at[g], (place.down, lon))
                backs[g, 1] = back.send(
                    col_out.at[g, pl.ds(0, 4)], col_in.at[g, pl.ds(0, 4)], (lat, place.east)
                )
                backs[g, 2] = back.send(
                    col_out.at[g, 4, pl.ds(0, 16)],
                    col_in.at[g, 4, pl.ds(0, 16)],
                    (lat, place.east),
                )
                backs[g, 3] = back.send(
                    col_out.at[g, 4, pl.ds(16, 16)],
                    col_in.at[g, 4, pl.ds(16, 16)],
                    (place.down, place.east),
                )
                backs[g, 4] = back.send(col_out.at[g, 5], col_in.at[g, 5], (place.down, place.east))
            if g == 0 and half == 0:
                send_rows(1)
            between[2 * g + half]()

    there.finish()
    for g in range(2):
        for part in range(1, 5):
            backs[g, part].wait_recv()
        for b in range(4):
            placed = dot(spread_ref[...], col_in[g, b])
            for side in range(2):
                add_rows(LEVELS[g][side], 144 + 96 * b, 96, placed[96 * side : 96 * side + 96])
        backs[g, 0].wait_recv()
        placed = dot(spread_ref[...], col_in[g, 4])
        for side in range(2):
            mine = placed[96 * side : 96 * side + 96]
            add_rows(LEVELS[g][side], 528, 48, mine[:48])
            above = row_in[g, 48 * side : 48 * side + 48, :].astype(F32)
            add_rows(LEVELS[g][side], 0, 48, mine[48:] + above)
        placed = dot(spread_ref[...], col_in[g, 5])
        for side in range(2):
            above = row_in[g, 96 + 96 * side : 192 + 96 * side, :].astype(F32)
            add_rows(LEVELS[g][side], 48, 96, placed[96 * side : 96 * side + 96] + above)
    back.finish()


def coarse_block(grid, gains, weights, tau, tables, work, loaded, gather):
    merge_gain, gain = gains
    wm, wc, ws = weights
    to_cells, from_cells, masks_ref, tail_ref, sums_ref = tables
    merged, coarse, x_ref, q_ref, k_ref, v_ref, mixed_ref, split, weight_ref = work
    for g in range(2):
        for b in range(3):
            cells = dot(to_cells[:, :192], grid[2 * g, pl.ds(192 * b, 192), :]) + dot(
                to_cells[:, 192:], grid[2 * g + 1, pl.ds(192 * b, 192), :]
            )
            parts = [cells[96 * n : 96 * n + 96] for n in range(4)]
            mean = sum(jnp.sum(part, axis=-1, keepdims=True) for part in parts) * (1 / 2048)
            parts = [part - mean for part in parts]
            spread = sum(jnp.sum(part * part, axis=-1, keepdims=True) for part in parts)
            factor = lax.rsqrt(spread * (1 / 2048) + 1e-05)
            for n in range(4):
                lanes = slice(512 * n, 512 * n + 512)
                normed = (parts[n] * factor * merge_gain[:, lanes]).astype(BF)
                for c in range(2):
                    at = (c * 2 + g) * 144 + b * 48
                    merged[at : at + 48, lanes] = normed[48 * c : 48 * c + 48]
    loaded[0].wait()
    for n in range(4):
        lanes = slice(256 * n, 256 * n + 256)
        coarse[:, lanes] = dot(merged[...], wm[:, lanes]).astype(BF)
        if n == 0:
            gather.fifth()
    for w in range(4):
        at = slice(144 * w, 144 * w + 144)
        x_ref[at, :] = norm_block(coarse[at, :].astype(F32), gain[...])
    gather.finish()
    for group in range(2):
        make_qkv(x_ref, wc, q_ref, k_ref, v_ref, tau, sums_ref[...], 1024, group)
        attend(
            q_ref, k_ref, v_ref, mixed_ref, group * 512, None, masks_ref, tail_ref, weight_ref
        )
    for n in range(4):
        lanes = slice(256 * n, 256 * n + 256)
        update = dot(mixed_ref[...], wc[:, 3072 + 256 * n : 3328 + 256 * n])
        coarse[:, lanes] = (coarse[:, lanes].astype(F32) + update).astype(BF)
    loaded[1].wait()
    for n in range(8):
        lanes = slice(256 * n, 256 * n + 256)
        split[:, lanes] = dot(coarse[...], ws[:, lanes]).astype(BF)
    for g in range(2):
        for b in range(3):
            parts = []
            for n in range(4):
                for c in range(2):
                    at = (c * 2 + g) * 144 + b * 48
                    parts.append(split[at : at + 48, 512 * n : 512 * n + 512])
            placed = dot(from_cells[...], jnp.concatenate(parts, axis=0))
            for side in range(2):
                here = grid.at[2 * g + side, pl.ds(192 * b, 192)]
                here[...] = (
                    here[...].astype(F32) + placed[192 * side : 192 * side + 192]
                ).astype(BF)


SCRATCH = {
    "grid": ((4, 576, 512), BF),
    "blocks": ((2, 6, 224, 512), BF),
    "picked": ((2, 6, 32, 512), BF),
    "row_out": ((2, 288, 512), BF),
    "col_out": ((2, 6, 32, 512), BF),
    "row_in": ((2, 288, 512), BF),
    "col_in": ((2, 6, 32, 512), BF),
    "x_fine": ((576, 512), BF),
    "q": ((576, 512), BF),
    "k": ((576, 512), BF),
    "v": ((576, 512), BF),
    "mixed_fine": ((576, 512), BF),
    "shifted": ((576, 512), BF),
    "bias": ((144, 256), F32),
    "merged": ((576, 2048), BF),
    "coarse": ((576, 1024), BF),
    "x_coarse": ((576, 1024), BF),
    "mixed_coarse": ((576, 1024), BF),
    "split": ((576, 2048), BF),
    "attention": ((576, 1536), BF),
    "coarse_weights": ((1024, 4096), BF),
}
SEMAPHORES = {
    "load": 40,
    "copy": 20,
    "there_send": 16,
    "there_recv": 16,
    "back_send": 10,
    "back_recv": 10,
    "gather_send": 20,
    "gather_recv": 20,
}


def kernel(lat_size, lon_size, names, *refs):
    count = len(names)
    given = dict(zip(names, refs[:count]))
    out = refs[count]
    held = dict(zip(names[3:], refs[count + 1 :]))
    rest = refs[count + 1 + count - 3 :]
    at = dict(zip(list(SCRATCH) + list(SEMAPHORES), rest))
    place = Place(lat_size, lon_size)
    grid, whole = at["grid"], at["coarse_weights"]
    start = pl.ds(pl.multiple_of(place.lon * 64, 16), 64)
    loads = {}

    def load(name, source, target):
        loads[name] = pltpu.make_async_copy(source, target, at["load"].at[len(loads)])
        loads[name].start()

    load("tokens", given["tokens"], grid)
    load("coarse_qkv", given["coarse_qkv"], whole.at[start, pl.ds(0, 3072)])
    load("coarse_proj", given["coarse_proj"], whole.at[start, pl.ds(3072, 1024)])
    for name in names[3:]:
        load(name, given[name], held[name])

    barrier = pltpu.get_barrier_semaphore()
    partners = place.halo + place.gather
    for device in partners:
        pl.semaphore_signal(barrier, inc=1, device_id=device, device_id_type=MESH)
    pl.semaphore_wait(barrier, len(partners))

    gather = Gather(place, whole, Mover(at["gather_send"], at["gather_recv"]))
    loads["coarse_qkv"].wait()
    loads["coarse_proj"].wait()
    loads["tokens"].wait()
    gather.start()
    late = ("merge_weight", "expand_weight")
    for name in names[3:]:
        if name not in late:
            loads[name].wait()

    fine_tables = [
        held[name]
        for name in ("windows", "windows_t", "spread", "pick", "differ", "masks", "tail", "sums")
    ]
    work = [
        at[name]
        for name in ("x_fine", "q", "k", "v", "mixed_fine", "shifted", "bias", "attention")
    ]
    comm = [at[name] for name in ("blocks", "picked", "row_out", "col_out", "row_in", "col_in")]
    comm += [(at["there_send"], at["there_recv"]), (at["back_send"], at["back_recv"])]
    nothing = lambda: None

    def fine(prefix, between):
        fine_block(
            grid,
            held[prefix + "_gain"],
            held[prefix + "_qkv"],
            held[prefix + "_proj"],
            held[prefix + "_tau"],
            place,
            fine_tables,
            work,
            comm,
            at["copy"],
            between,
        )

    fine("enc", (gather.second, gather.third, nothing, gather.fourth))
    coarse_block(
        grid,
        (held["merge_gain"], held["coarse_gain"]),
        (held["merge_weight"], whole, held["expand_weight"]),
        held["coarse_tau"],
        [held[name] for name in ("cells", "cells_t", "masks", "tail", "sums")],
        [
            at[name]
            for name in (
                "merged",
                "coarse",
                "x_coarse",
                "q",
                "k",
                "v",
                "mixed_coarse",
                "split",
                "attention",
            )
        ],
        [loads[name] for name in late],
        gather,
    )
    gather.mover.finish()
    fine("dec", (nothing,) * 4)
    store = pltpu.make_async_copy(grid, out, at["load"].at[0])
    store.start()
    store.wait()


def publish_kernel(source, target, sem):
    copies = []
    for level in range(4):
        for part in range(4):
            rows = pl.ds(144 * part, 144)
            copy = pltpu.make_async_copy(
                source.at[level, rows], target.at[level, rows], sem.at[level * 4 + part]
            )
            copy.start()
            copies.append(copy)
    for copy in copies:
        copy.wait()


def publish(values):
    return pl.pallas_call(
        publish_kernel,
        out_shape=jax.ShapeDtypeStruct(values.shape, values.dtype),
        in_specs=[HBM],
        out_specs=HBM,
        scratch_shapes=[pltpu.SemaphoreType.DMA((16,))],
        compiler_params=pltpu.CompilerParams(vmem_limit_bytes=60 << 20),
        name="publish",
    )(values)


def local(
    tokens,
    enc_gain,
    enc_qkv,
    enc_proj,
    enc_tau,
    merge_gain,
    merge_weight,
    coarse_gain,
    coarse_qkv,
    coarse_proj,
    coarse_tau,
    expand_weight,
    dec_gain,
    dec_qkv,
    dec_proj,
    dec_tau,
):
    table = lambda values: jnp.asarray(values, BF)
    row = lambda values: values.reshape(1, -1)
    windows, cells = block_to_windows(), grid_to_cells()
    given = {
        "tokens": tokens.reshape(4, 576, 512),
        "coarse_qkv": coarse_qkv,
        "coarse_proj": coarse_proj,
        "enc_gain": row(enc_gain),
        "enc_tau": row(enc_tau),
        "pick": table(grid_to_beside()),
        "windows": table(windows),
        "enc_qkv": enc_qkv,
        "sums": table(head_sums()),
        "masks": table(half_masks()),
        "tail": table(tail_mask()),
        "enc_proj": enc_proj,
        "windows_t": table(windows.T),
        "spread": table(beside_to_block()),
        "differ": jnp.asarray(differences()),
        "merge_gain": row(merge_gain),
        "coarse_gain": row(coarse_gain),
        "coarse_tau": row(coarse_tau),
        "dec_gain": row(dec_gain),
        "dec_tau": row(dec_tau),
        "dec_qkv": dec_qkv,
        "dec_proj": dec_proj,
        "cells": table(cells),
        "cells_t": table(cells.T),
        "merge_weight": merge_weight,
        "expand_weight": expand_weight,
    }
    names = tuple(given)
    scratch = [pltpu.VMEM(given[name].shape, given[name].dtype) for name in names[3:]]
    scratch += [pltpu.VMEM(shape, dtype) for shape, dtype in SCRATCH.values()]
    scratch += [pltpu.SemaphoreType.DMA((n,)) for n in SEMAPHORES.values()]
    decoded = pl.pallas_call(
        functools.partial(kernel, lax.axis_size("lat"), lax.axis_size("lon"), names),
        out_shape=jax.ShapeDtypeStruct((4, 576, 512), BF),
        in_specs=[HBM] * len(names),
        out_specs=HBM,
        scratch_shapes=scratch,
        compiler_params=pltpu.CompilerParams(
            collective_id=0, has_side_effects=True, vmem_limit_bytes=60 << 20
        ),
        cost_estimate=pl.CostEstimate(
            flops=35_000_000_000, bytes_accessed=30_000_000, transcendentals=8_000_000
        ),
        name="blocks",
    )(*given.values())
    return publish(decoded).reshape(4, 24, 24, 512)


def solution(mesh):
    placed = (
        P(None, "lat", "lon", None),
        P(),
        P(),
        P(),
        P(),
        P(),
        P(),
        P(),
        P("lon", None),
        P("lon", None),
        P(),
        P(),
        P(),
        P(),
        P(),
        P(),
    )
    return jax.shard_map(
        local, mesh=mesh, in_specs=placed, out_specs=P(None, "lat", "lon", None), check_vma=False
    )
```

```python
import functools

import jax
import jax.numpy as jnp
import numpy as np
from jax import lax
from jax.experimental import pallas as pl
from jax.experimental.pallas import tpu as pltpu
from jax.sharding import PartitionSpec as P

MESH = pl.DeviceIdType.MESH
BF = jnp.bfloat16
F32 = jnp.float32
LOG2E = 1.4426950408889634
NT = (((1,), (1,)), ((), ()))
HBM = pl.BlockSpec(memory_space=pltpu.HBM)
LEVELS = ((1, 2), (3, 0))


def dot(a, b):
    return jnp.dot(a, b, preferred_element_type=F32)


def beside_at(level, row, column):
    return (row // 2) * 16 + level * 6 + (row % 2) * 3 + column


def block_to_windows():
    table = np.zeros((192, 224), np.float32)
    for w in range(4):
        for level in range(2):
            for row in range(4):
                for c in range(6):
                    column = 3 + 6 * w + c
                    if column < 24:
                        source = level * 96 + row * 24 + column
                    else:
                        source = 192 + beside_at(level, row, column - 24)
                    table[w * 48 + level * 24 + row * 6 + c, source] = 1
    return table


def beside_to_block():
    table = np.zeros((192, 32), np.float32)
    for level in range(2):
        for row in range(4):
            for c in range(3):
                table[level * 96 + row * 24 + c, beside_at(level, row, c)] = 1
    return table


def block_row(block, row):
    if block < 4:
        return 6 + 4 * block + row
    if block == 4:
        return 22 + row if row < 2 else row - 2
    return 2 + row


def grid_to_beside():
    table = np.zeros((2, 192, 576), np.float32)
    for block in range(6):
        for level in range(2):
            for row in range(4):
                for c in range(3):
                    at = block * 32 + beside_at(level, row, c)
                    table[level, at, block_row(block, row) * 24 + c] = 1
    return table


def grid_to_cells():
    table = np.zeros((384, 384), np.float32)
    for pr in range(2):
        for pc in range(2):
            for cw in range(2):
                for level in range(2):
                    for i in range(4):
                        for j in range(6):
                            at = (pr * 2 + pc) * 96 + cw * 48 + level * 24 + i * 6 + j
                            source = level * 192 + (2 * i + pr) * 24 + 2 * (6 * cw + j) + pc
                            table[at, source] = 1
    return table


def differences():
    token = np.arange(144)
    level = (token // 24) % 2
    low = ((token // 48) * 4 + (token % 24) // 6) >= 6
    keys = np.concatenate([token[:128], np.tile(token[128:], 8)])
    by_level = (level[:, None] != level[keys][None]).astype(np.float32)
    by_row = (low[:, None] != low[keys][None]).astype(np.float32)
    return np.stack([by_level, by_row]) * np.float32(-1e30)


def half_masks():
    left = np.zeros((2, 128, 128), np.float32)
    left[0, :, :64] = 1
    left[1, :, 64:] = 1
    return left


def tail_mask():
    return (np.arange(128)[:, None] // 16 == np.arange(512)[None] // 64).astype(np.float32)


def head_sums():
    at = np.arange(256) // 64
    return (at[:, None] == at[None]).astype(np.float32)


def norm_block(values, gain):
    mean = jnp.mean(values, axis=-1, keepdims=True)
    center = values - mean
    spread = jnp.mean(center * center, axis=-1, keepdims=True)
    return (center * lax.rsqrt(spread + 1e-05) * gain).astype(BF)


def head_scale(tau_ref, first):
    at = lax.broadcasted_iota(jnp.int32, (1, 256), 1) // 64
    scale = jnp.zeros((1, 256), F32)
    for h in range(4):
        scale = jnp.where(at == h, tau_ref[:, first + h : first + h + 1], scale)
    return scale * LOG2E


def make_qkv(x_ref, w_ref, q_ref, k_ref, v_ref, tau_ref, sums, width, group):
    def product(target, part, half):
        at = part * width + group * 512 + half * 256
        target[:, half * 256 : half * 256 + 256] = dot(x_ref[...], w_ref[:, at : at + 256]).astype(BF)

    def unit(target, half, scaled):
        lanes = slice(half * 256, half * 256 + 256)
        values = target[:, lanes]
        factor = lax.rsqrt(dot(values * values, sums) + 1e-06)
        if scaled:
            factor = factor * head_scale(tau_ref, group * 8 + half * 4)
        target[:, lanes] = (values.astype(F32) * factor).astype(BF)

    product(q_ref, 0, 0)
    product(q_ref, 0, 1)
    unit(q_ref, 0, True)
    product(k_ref, 1, 0)
    unit(q_ref, 1, True)
    product(k_ref, 1, 1)
    unit(k_ref, 0, False)
    product(v_ref, 2, 0)
    unit(k_ref, 1, False)
    product(v_ref, 2, 1)


def attend(
    q_ref, k_ref, v_ref, out_ref, out_at, bias_ref, masks_ref, tail_ref, weight_ref, windows
):
    left, right = masks_ref[0], masks_ref[1]
    tail = tail_ref[...]

    def weights(score, bias):
        return jnp.exp2(score if bias is None else score + bias).astype(BF)

    bias_main = bias_tail = None
    if bias_ref is not None:
        bias_main = jnp.concatenate([bias_ref[:, :128], bias_ref[:, :128]], axis=1)
        bias_tail = bias_ref[:, 128:]
    for w in range(windows):
        row = w * 144
        rows = slice(row, row + 144)
        q = q_ref[rows, :]
        k_tails = jnp.concatenate([k_ref[row + 128 : row + 144, :]] * 8, axis=0) * tail
        score = lax.dot_general(q, k_tails, NT, preferred_element_type=F32)
        weight_tail = weights(score, bias_tail)
        for pair in range(4):
            lanes = slice(pair * 128, pair * 128 + 128)
            k = k_ref[row : row + 128, lanes]
            k_pair = jnp.concatenate([k * left, k * right], axis=0)
            score = lax.dot_general(q[:, lanes], k_pair, NT, preferred_element_type=F32)
            weight_ref[rows, pair * 384 : pair * 384 + 256] = weights(score, bias_main)
            weight_ref[rows, pair * 384 + 256 : pair * 384 + 384] = weight_tail
    for w in range(windows):
        row = w * 144
        rows = slice(row, row + 144)
        v_tails = jnp.concatenate([v_ref[row + 128 : row + 144, :]] * 8, axis=0) * tail
        for pair in range(4):
            lanes = slice(pair * 128, pair * 128 + 128)
            v = v_ref[row : row + 128, lanes]
            v_pair = jnp.concatenate(
                [
                    jnp.concatenate([v * left, left], axis=1),
                    jnp.concatenate([v * right, right], axis=1),
                    jnp.concatenate([v_tails[:, lanes], tail[:, lanes]], axis=1),
                ],
                axis=0,
            )
            both = dot(weight_ref[rows, pair * 384 : pair * 384 + 384], v_pair)
            mixed = (both[:, :128] / both[:, 128:]).astype(BF)
            out_ref[rows, out_at + pair * 128 : out_at + pair * 128 + 128] = mixed


class Mover:
    def __init__(self, send_sem, recv_sem):
        self.send_sem, self.recv_sem = send_sem, recv_sem
        self.count = 0
        self.sent = []

    def send(self, source, target, device):
        copy = pltpu.make_async_remote_copy(
            src_ref=source,
            dst_ref=target,
            send_sem=self.send_sem.at[self.count],
            recv_sem=self.recv_sem.at[self.count],
            device_id=device,
            device_id_type=MESH,
        )
        copy.start()
        self.count += 1
        self.sent.append(copy)
        return copy

    def finish(self):
        for copy in self.sent:
            copy.wait_send()


class Place:
    def __init__(self, lat_size, lon_size):
        lat, lon = lax.axis_index("lat"), lax.axis_index("lon")
        self.lat, self.lon = lat, lon
        self.up, self.down = lax.rem(lat + lat_size - 1, lat_size), lax.rem(lat + 1, lat_size)
        self.west, self.east = lax.rem(lon + lon_size - 1, lon_size), lax.rem(lon + 1, lon_size)
        self.last = (lat == lat_size - 1).astype(F32)
        self.x_next, self.x_last = lax.rem(lon + 4, 16), lax.rem(lon + 12, 16)
        self.x_far = lax.rem(lon + 8, 16)
        self.mate = lon + 1 - 2 * lax.rem(lon, 2)
        self.across = lon + 2 - 4 * lax.rem(lon // 2, 2)
        self.z = lat // 2
        self.other_z = tuple(lax.rem(lat + 2 * n, 8) for n in (1, 3, 2))
        self.halo = (
            (self.up, lon),
            (self.down, lon),
            (lat, self.west),
            (lat, self.east),
            (self.up, self.west),
            (self.down, self.east),
        )
        self.gather = (
            (lat, self.x_next),
            (lat, self.x_last),
            (lat, self.mate),
            (lat, self.across),
        ) + tuple((other, lon) for other in self.other_z)


class Gather:
    def __init__(self, place, rows, columns, mover):
        self.place, self.rows, self.columns, self.mover = place, rows, columns, mover
        self.from_mate = []

    def part(self, owner, first, size):
        return self.rows.at[pl.ds(pl.multiple_of(owner * 64 + first, 16), size), self.columns]

    def send(self, owner, first, size, device):
        part = self.part(owner, first, size)
        return self.mover.send(part, part, device)

    def to_mate(self, owner):
        place = self.place
        self.from_mate.append(self.send(owner, 0, 64, (place.lat, place.mate)))

    def along_x(self, owner):
        place = self.place
        return (
            self.send(owner, 0, 64, (place.lat, place.x_next)),
            self.send(owner, 0, 64, (place.lat, place.x_last)),
        )

    def relay_x(self, before, after):
        place = self.place
        return (
            self.send(before, 0, 32, (place.lat, place.x_next)),
            self.send(after, 32, 32, (place.lat, place.x_last)),
        )

    def start(self):
        place = self.place
        self.near = self.along_x(place.lon)
        quarter = pl.multiple_of(place.z * 16, 16)
        self.quarter = self.send(place.lon, quarter, 16, (place.lat, place.across))
        self.to_mate(place.lon)

    def second(self):
        place = self.place
        for copy in self.near:
            copy.wait_recv()
        self.far = self.relay_x(place.x_last, place.x_next)
        self.quarter.wait_recv()
        quarter = pl.multiple_of(place.z * 16, 16)
        self.quarters = [
            self.send(place.across, quarter, 16, (other, place.lon)) for other in place.other_z
        ]
        self.to_mate(place.x_last)
        self.to_mate(place.x_next)

    def across_of(self, lon):
        return lon + 2 - 4 * lax.rem(lon // 2, 2)

    def third(self):
        place = self.place
        for copy in self.quarters:
            copy.wait_recv()
        self.near = self.along_x(place.across)
        for copy in self.far:
            copy.wait_recv()
        self.to_mate(place.x_far)
        self.to_mate(place.across)

    def fourth(self):
        place = self.place
        for copy in self.near:
            copy.wait_recv()
        before, after = self.across_of(place.x_last), self.across_of(place.x_next)
        self.far = self.relay_x(before, after)
        self.to_mate(before)
        self.to_mate(after)

    def fifth(self):
        for copy in self.far:
            copy.wait_recv()
        self.to_mate(self.across_of(self.place.x_far))

    def finish(self):
        for copy in self.from_mate:
            copy.wait_recv()


class Fine:
    def __init__(self, grid, gain, wq, wp, tau, place, tables, work, comm, copy_sem):
        self.grid, self.gain, self.wq, self.wp, self.tau = grid, gain, wq, wp, tau
        self.place, self.tables, self.work = place, tables, work
        (
            self.blocks,
            self.picked,
            self.row_out,
            self.col_out,
            self.row_in,
            self.col_in,
            there_sems,
            back_sems,
        ) = comm
        self.there, self.back = Mover(*there_sems), Mover(*back_sems)
        self.copy_sem = copy_sem
        self.rows, self.columns, self.row_backs, self.col_backs = {}, {}, {}, {}
        self.own = []

    def send_rows(self, g, side):
        level, target = LEVELS[g][side], (self.place.up, self.place.lon)
        grid, blocks = self.grid, self.blocks
        self.rows[g, side] = (
            self.there.send(
                grid.at[level, pl.ds(0, 48)], blocks.at[g, 4, pl.ds(96 * side + 48, 48)], target
            ),
            self.there.send(
                grid.at[level, pl.ds(48, 96)], blocks.at[g, 5, pl.ds(96 * side, 96)], target
            ),
        )

    def send_columns(self, g):
        pick, grid = self.tables[3], self.grid
        picked, blocks, place = self.picked, self.blocks, self.place
        picks = dot(pick[0], grid[LEVELS[g][0]]) + dot(pick[1], grid[LEVELS[g][1]])
        for b in range(6):
            picked[g, b] = picks[32 * b : 32 * b + 32].astype(BF)
        beside, above = (place.lat, place.west), (place.up, place.west)
        send = self.there.send
        near, far = pl.ds(192, 16), pl.ds(208, 16)
        both = pl.ds(192, 32)
        self.columns[g] = (
            send(picked.at[g, pl.ds(0, 4)], blocks.at[g, pl.ds(0, 4), both], beside),
            send(picked.at[g, 4, pl.ds(0, 16)], blocks.at[g, 4, near], beside),
            send(picked.at[g, 4, pl.ds(16, 16)], blocks.at[g, 4, far], above),
            send(picked.at[g, 5], blocks.at[g, 5, both], above),
        )

    def place_own(self, g, side):
        level = LEVELS[g][side]
        for b in range(5):
            size = 96 if b < 4 else 48
            copy = pltpu.make_async_copy(
                self.grid.at[level, pl.ds(144 + 96 * b, size)],
                self.blocks.at[g, b, pl.ds(96 * side, size)],
                self.copy_sem.at[(g * 2 + side) * 5 + b],
            )
            copy.start()
            self.own.append(copy)

    def add_rows(self, level, at, size, values):
        grid = self.grid
        grid[level, pl.ds(at, size), :] = (
            grid[level, pl.ds(at, size), :].astype(F32) + values
        ).astype(BF)

    def wait_for(self, g, half):
        if half == 0:
            self.columns[g][0].wait_recv()
            return
        for copy in self.columns[g][1:] + self.rows[g, 0] + self.rows[g, 1]:
            copy.wait_recv()

    def unit(self, g, half):
        to_windows, from_windows, _, _, diff_ref, masks_ref, tail_ref, sums_ref = self.tables
        x_ref, q_ref, k_ref, v_ref, mixed_ref, shifted_ref, bias_ref, weight_ref = self.work
        for b in range(3):
            tokens_in = dot(to_windows[...], self.blocks[g, 3 * half + b])
            normed = norm_block(tokens_in, self.gain[...])
            for w in range(4):
                at = w * 144 + b * 48
                x_ref[at : at + 48, :] = normed[48 * w : 48 * w + 48]
        make_qkv(x_ref, self.wq, q_ref, k_ref, v_ref, self.tau, sums_ref[...], 512, 0)
        masked = g == 1 or half == 1
        if masked:
            bias = jnp.zeros((144, 256), F32)
            if g == 1:
                bias = bias + diff_ref[0]
            if half == 1:
                bias = bias + diff_ref[1] * self.place.last
            bias_ref[...] = bias
        attend(
            q_ref,
            k_ref,
            v_ref,
            mixed_ref,
            0,
            bias_ref if masked else None,
            masks_ref,
            tail_ref,
            weight_ref,
            4,
        )
        shifted_ref[...] = dot(mixed_ref[...], self.wp[...]).astype(BF)
        for b in range(3):
            index = 3 * half + b
            parts = [shifted_ref[w * 144 + b * 48 : w * 144 + b * 48 + 48, :] for w in range(4)]
            placed = dot(from_windows[...], jnp.concatenate(parts, axis=0))
            self.col_out[g, index] = placed[192:224].astype(BF)
            for side in range(2):
                level = LEVELS[g][side]
                mine = placed[96 * side : 96 * side + 96]
                if index < 4:
                    self.add_rows(level, 144 + 96 * index, 96, mine)
                elif index == 4:
                    self.add_rows(level, 528, 48, mine[:48])
                    self.row_out[g, 144 * side : 144 * side + 48, :] = mine[48:].astype(BF)
                else:
                    self.row_out[g, 144 * side + 48 : 144 * side + 144, :] = mine.astype(BF)

    def return_rows(self, g, side):
        part = pl.ds(144 * side, 144)
        self.row_backs[g, side] = self.back.send(
            self.row_out.at[g, part], self.row_in.at[g, part], (self.place.down, self.place.lon)
        )

    def return_columns(self, g):
        place, send = self.place, self.back.send
        beside, below = (place.lat, place.east), (place.down, place.east)

        def one(part, device):
            return send(self.col_out.at[(g, *part)], self.col_in.at[(g, *part)], device)

        self.col_backs[g] = (
            one((pl.ds(0, 4),), beside),
            one((4, pl.ds(0, 16)), beside),
            one((4, pl.ds(16, 16)), below),
            one((5,), below),
        )

    def take_columns(self, g):
        spread = self.tables[2]
        for copy in self.col_backs[g]:
            copy.wait_recv()
        for b in range(6):
            placed = dot(spread[...], self.col_in[g, b])
            for side in range(2):
                level, mine = LEVELS[g][side], placed[96 * side : 96 * side + 96]
                if b < 4:
                    self.add_rows(level, 144 + 96 * b, 96, mine)
                elif b == 4:
                    self.add_rows(level, 528, 48, mine[:48])
                    self.add_rows(level, 0, 48, mine[48:])
                else:
                    self.add_rows(level, 48, 96, mine)

    def take_rows(self, g, side):
        self.row_backs[g, side].wait_recv()
        above = self.row_in[g, 144 * side : 144 * side + 144, :].astype(F32)
        self.add_rows(LEVELS[g][side], 0, 144, above)

    def units(self, between):
        for copy in self.own:
            copy.wait()
        between[0]()
        self.unit(0, 0)
        between[1]()
        self.wait_for(0, 1)
        self.unit(0, 1)
        self.return_rows(0, 0)
        self.return_rows(0, 1)
        self.return_columns(0)
        between[2]()
        self.wait_for(1, 0)
        self.wait_for(1, 1)
        self.unit(1, 1)
        self.return_rows(1, 1)
        self.return_rows(1, 0)
        self.unit(1, 0)
        self.return_columns(1)
        self.there.finish()


def coarse_pass(g, grid, gains, weights, tau, tables, work, loaded, gather_qkv, gather_proj):
    merge_gain, gain = gains
    wm, wc, ws = weights
    to_cells, from_cells, masks_ref, tail_ref, sums_ref = tables
    merged, coarse, x_ref, q_ref, k_ref, v_ref, mixed_ref, split, weight_ref = work
    for b in range(3):
        cells = dot(to_cells[:, :192], grid[2 * g, pl.ds(192 * b, 192), :]) + dot(
            to_cells[:, 192:], grid[2 * g + 1, pl.ds(192 * b, 192), :]
        )
        parts = [cells[96 * n : 96 * n + 96] for n in range(4)]
        mean = sum(jnp.sum(part, axis=-1, keepdims=True) for part in parts) * (1 / 2048)
        parts = [part - mean for part in parts]
        spread = sum(jnp.sum(part * part, axis=-1, keepdims=True) for part in parts)
        factor = lax.rsqrt(spread * (1 / 2048) + 1e-05)
        for n in range(4):
            lanes = slice(512 * n, 512 * n + 512)
            normed = (parts[n] * factor * merge_gain[:, lanes]).astype(BF)
            for c in range(2):
                at = c * 144 + b * 48
                merged[at : at + 48, lanes] = normed[48 * c : 48 * c + 48]
    if g == 0:
        loaded[0].wait()
    for n in range(4):
        lanes = slice(256 * n, 256 * n + 256)
        coarse[:, lanes] = dot(merged[...], wm[:, lanes]).astype(BF)
        if g == 0 and n == 0:
            gather_qkv.fifth()
            gather_proj.third()
    for w in range(2):
        at = slice(144 * w, 144 * w + 144)
        x_ref[at, :] = norm_block(coarse[at, :].astype(F32), gain[...])
    if g == 0:
        gather_qkv.finish()
    for group in range(2):
        make_qkv(x_ref, wc, q_ref, k_ref, v_ref, tau, sums_ref[...], 1024, group)
        attend(
            q_ref,
            k_ref,
            v_ref,
            mixed_ref,
            group * 512,
            None,
            masks_ref,
            tail_ref,
            weight_ref,
            2,
        )
        if g == 0 and group == 0:
            gather_proj.fourth()
    if g == 0:
        gather_proj.fifth()
        gather_proj.finish()
    for n in range(4):
        lanes = slice(256 * n, 256 * n + 256)
        update = dot(mixed_ref[...], wc[:, 3072 + 256 * n : 3328 + 256 * n])
        coarse[:, lanes] = (coarse[:, lanes].astype(F32) + update).astype(BF)
    if g == 0:
        loaded[1].wait()
    for n in range(8):
        lanes = slice(256 * n, 256 * n + 256)
        split[:, lanes] = dot(coarse[...], ws[:, lanes]).astype(BF)
    for b in range(3):
        parts = []
        for n in range(4):
            for c in range(2):
                at = c * 144 + b * 48
                parts.append(split[at : at + 48, 512 * n : 512 * n + 512])
        placed = dot(from_cells[...], jnp.concatenate(parts, axis=0))
        for side in range(2):
            here = grid.at[2 * g + side, pl.ds(192 * b, 192)]
            here[...] = (here[...].astype(F32) + placed[192 * side : 192 * side + 192]).astype(BF)


SCRATCH = {
    "grid": ((4, 576, 512), BF),
    "blocks": ((2, 6, 224, 512), BF),
    "picked": ((2, 6, 32, 512), BF),
    "row_out": ((2, 288, 512), BF),
    "col_out": ((2, 6, 32, 512), BF),
    "row_in": ((2, 288, 512), BF),
    "col_in": ((2, 6, 32, 512), BF),
    "x_fine": ((576, 512), BF),
    "q": ((576, 512), BF),
    "k": ((576, 512), BF),
    "v": ((576, 512), BF),
    "mixed_fine": ((576, 512), BF),
    "shifted": ((576, 512), BF),
    "bias": ((144, 256), F32),
    "merged": ((288, 2048), BF),
    "coarse": ((288, 1024), BF),
    "x_coarse": ((288, 1024), BF),
    "mixed_coarse": ((288, 1024), BF),
    "split": ((288, 2048), BF),
    "attention": ((576, 1536), BF),
    "coarse_weights": ((1024, 4096), BF),
}
SEMAPHORES = {
    "load": 40,
    "copy": 20,
    "there_send": 16,
    "there_recv": 16,
    "back_send": 12,
    "back_recv": 12,
    "gather_send": 40,
    "gather_recv": 40,
}


def kernel(lat_size, lon_size, names, *refs):
    count = len(names)
    given = dict(zip(names, refs[:count]))
    out = refs[count]
    held = dict(zip(names[3:], refs[count + 1 :]))
    rest = refs[count + 1 + count - 3 :]
    at = dict(zip(list(SCRATCH) + list(SEMAPHORES), rest))
    place = Place(lat_size, lon_size)
    grid, whole = at["grid"], at["coarse_weights"]
    start = pl.ds(pl.multiple_of(place.lon * 64, 16), 64)
    loads = {}

    def load(name, source, target):
        loads[name] = pltpu.make_async_copy(source, target, at["load"].at[len(loads)])
        loads[name].start()

    load("tokens", given["tokens"], grid)
    load("coarse_qkv", given["coarse_qkv"], whole.at[start, pl.ds(0, 3072)])
    load("coarse_proj", given["coarse_proj"], whole.at[start, pl.ds(3072, 1024)])
    for name in names[3:]:
        load(name, given[name], held[name])

    barrier = pltpu.get_barrier_semaphore()
    partners = place.halo + place.gather
    for device in partners:
        pl.semaphore_signal(barrier, inc=1, device_id=device, device_id_type=MESH)
    pl.semaphore_wait(barrier, len(partners))

    mover = Mover(at["gather_send"], at["gather_recv"])
    gather_qkv = Gather(place, whole, pl.ds(0, 3072), mover)
    gather_proj = Gather(place, whole, pl.ds(3072, 1024), mover)
    late = ("merge_weight", "expand_weight")
    loads["tokens"].wait()

    fine_tables = [
        held[name]
        for name in ("windows", "windows_t", "spread", "pick", "differ", "masks", "tail", "sums")
    ]
    work = [
        at[name]
        for name in ("x_fine", "q", "k", "v", "mixed_fine", "shifted", "bias", "attention")
    ]
    comm = [at[name] for name in ("blocks", "picked", "row_out", "col_out", "row_in", "col_in")]
    comm += [(at["there_send"], at["there_recv"]), (at["back_send"], at["back_recv"])]

    def fine(prefix):
        return Fine(
            grid,
            held[prefix + "_gain"],
            held[prefix + "_qkv"],
            held[prefix + "_proj"],
            held[prefix + "_tau"],
            place,
            fine_tables,
            work,
            comm,
            at["copy"],
        )

    def coarse(g):
        half = pl.ds(0, 288)
        coarse_pass(
            g,
            grid,
            (held["merge_gain"], held["coarse_gain"]),
            (held["merge_weight"], whole, held["expand_weight"]),
            held["coarse_tau"],
            [held[name] for name in ("cells", "cells_t", "masks", "tail", "sums")],
            [at[name] for name in ("merged", "coarse", "x_coarse")]
            + [at[name].at[half] for name in ("q", "k", "v")]
            + [at[name] for name in ("mixed_coarse", "split", "attention")],
            [loads[name] for name in late],
            gather_qkv,
            gather_proj,
        )

    first = fine("enc")
    first.send_rows(0, 0)
    first.send_rows(0, 1)
    for g in range(2):
        for side in range(2):
            first.place_own(g, side)
    loads["pick"].wait()
    first.send_columns(0)
    loads["coarse_qkv"].wait()
    loads["coarse_proj"].wait()
    gather_qkv.start()
    first.send_columns(1)
    for name in names[3:]:
        if name not in late + ("pick",) and not name.startswith("dec_"):
            loads[name].wait()

    def before_first():
        first.wait_for(0, 0)
        first.send_rows(1, 1)
        first.send_rows(1, 0)

    def after_second():
        gather_qkv.third()
        gather_proj.start()

    first.units((before_first, gather_qkv.second, after_second))
    gather_qkv.fourth()
    gather_proj.second()
    first.take_columns(0)
    first.take_columns(1)
    first.take_rows(0, 0)
    first.take_rows(0, 1)
    first.take_rows(1, 1)
    coarse(0)
    second = fine("dec")
    for name in ("dec_gain", "dec_tau", "dec_qkv", "dec_proj"):
        loads[name].wait()
    second.send_rows(0, 0)
    second.send_rows(1, 1)
    second.place_own(0, 0)
    second.place_own(1, 1)
    first.take_rows(1, 0)
    first.back.finish()
    coarse(1)
    second.send_rows(0, 1)
    second.send_columns(0)
    second.send_columns(1)
    second.send_rows(1, 0)
    second.place_own(0, 1)
    second.place_own(1, 0)
    mover.finish()
    nothing = lambda: None
    second.units((lambda: second.wait_for(0, 0), nothing, nothing))
    for g in range(2):
        second.take_columns(g)
        for side in range(2):
            second.take_rows(g, side)
    second.back.finish()
    store = pltpu.make_async_copy(grid, out, at["load"].at[0])
    store.start()
    store.wait()


def publish_kernel(source, target, held, load_sem, store_sem):
    loads, stores = [], []
    for level in range(4):
        for part in range(2):
            rows, at = pl.ds(288 * part, 288), level * 2 + part
            here = held.at[level, rows]
            loads.append(pltpu.make_async_copy(source.at[level, rows], here, load_sem.at[at]))
            stores.append(pltpu.make_async_copy(here, target.at[level, rows], store_sem.at[at]))
            loads[-1].start()
    for load, store in zip(loads, stores):
        load.wait()
        store.start()
    for store in stores:
        store.wait()


def publish(values):
    return pl.pallas_call(
        publish_kernel,
        out_shape=jax.ShapeDtypeStruct(values.shape, values.dtype),
        in_specs=[HBM],
        out_specs=HBM,
        scratch_shapes=[
            pltpu.VMEM(values.shape, values.dtype),
            pltpu.SemaphoreType.DMA((8,)),
            pltpu.SemaphoreType.DMA((8,)),
        ],
        compiler_params=pltpu.CompilerParams(vmem_limit_bytes=60 << 20),
        name="publish",
    )(values)


def local(
    tokens,
    enc_gain,
    enc_qkv,
    enc_proj,
    enc_tau,
    merge_gain,
    merge_weight,
    coarse_gain,
    coarse_qkv,
    coarse_proj,
    coarse_tau,
    expand_weight,
    dec_gain,
    dec_qkv,
    dec_proj,
    dec_tau,
):
    table = lambda values: jnp.asarray(values, BF)
    row = lambda values: values.reshape(1, -1)
    windows, cells = block_to_windows(), grid_to_cells()
    given = {
        "tokens": tokens.reshape(4, 576, 512),
        "coarse_qkv": coarse_qkv,
        "coarse_proj": coarse_proj,
        "enc_gain": row(enc_gain),
        "enc_tau": row(enc_tau),
        "pick": table(grid_to_beside()),
        "windows": table(windows),
        "enc_qkv": enc_qkv,
        "sums": table(head_sums()),
        "masks": table(half_masks()),
        "tail": table(tail_mask()),
        "enc_proj": enc_proj,
        "windows_t": table(windows.T),
        "spread": table(beside_to_block()),
        "differ": jnp.asarray(differences()),
        "merge_gain": row(merge_gain),
        "coarse_gain": row(coarse_gain),
        "coarse_tau": row(coarse_tau),
        "dec_gain": row(dec_gain),
        "dec_tau": row(dec_tau),
        "dec_qkv": dec_qkv,
        "dec_proj": dec_proj,
        "cells": table(cells),
        "cells_t": table(cells.T),
        "merge_weight": merge_weight,
        "expand_weight": expand_weight,
    }
    names = tuple(given)
    scratch = [pltpu.VMEM(given[name].shape, given[name].dtype) for name in names[3:]]
    scratch += [pltpu.VMEM(shape, dtype) for shape, dtype in SCRATCH.values()]
    scratch += [pltpu.SemaphoreType.DMA((n,)) for n in SEMAPHORES.values()]
    decoded = pl.pallas_call(
        functools.partial(kernel, lax.axis_size("lat"), lax.axis_size("lon"), names),
        out_shape=jax.ShapeDtypeStruct((4, 576, 512), BF),
        in_specs=[HBM] * len(names),
        out_specs=HBM,
        scratch_shapes=scratch,
        compiler_params=pltpu.CompilerParams(
            collective_id=0, has_side_effects=True, vmem_limit_bytes=60 << 20
        ),
        cost_estimate=pl.CostEstimate(
            flops=35_000_000_000, bytes_accessed=30_000_000, transcendentals=8_000_000
        ),
        name="blocks",
    )(*given.values())
    return publish(decoded).reshape(4, 24, 24, 512)


def solution(mesh):
    placed = (
        P(None, "lat", "lon", None),
        P(),
        P(),
        P(),
        P(),
        P(),
        P(),
        P(),
        P("lon", None),
        P("lon", None),
        P(),
        P(),
        P(),
        P(),
        P(),
        P(),
    )
    return jax.shard_map(
        local, mesh=mesh, in_specs=placed, out_specs=P(None, "lat", "lon", None), check_vma=False
    )
```

```python
import functools

import jax
import jax.numpy as jnp
import numpy as np
from jax import lax
from jax.experimental import pallas as pl
from jax.experimental.pallas import tpu as pltpu
from jax.sharding import PartitionSpec as P

MESH = pl.DeviceIdType.MESH
BF = jnp.bfloat16
F32 = jnp.float32
LOG2E = 1.4426950408889634
NT = (((1,), (1,)), ((), ()))
HBM = pl.BlockSpec(memory_space=pltpu.HBM)
LEVELS = ((1, 2), (3, 0))


def dot(a, b):
    return jnp.dot(a, b, preferred_element_type=F32)


def beside_at(level, row, column):
    return (row // 2) * 16 + level * 6 + (row % 2) * 3 + column


def block_to_windows():
    table = np.zeros((192, 224), np.float32)
    for w in range(4):
        for level in range(2):
            for row in range(4):
                for c in range(6):
                    column = 3 + 6 * w + c
                    if column < 24:
                        source = level * 96 + row * 24 + column
                    else:
                        source = 192 + beside_at(level, row, column - 24)
                    table[w * 48 + level * 24 + row * 6 + c, source] = 1
    return table


def beside_to_block():
    table = np.zeros((192, 32), np.float32)
    for level in range(2):
        for row in range(4):
            for c in range(3):
                table[level * 96 + row * 24 + c, beside_at(level, row, c)] = 1
    return table


def block_row(block, row):
    if block < 4:
        return 6 + 4 * block + row
    if block == 4:
        return 22 + row if row < 2 else row - 2
    return 2 + row


def grid_to_beside():
    table = np.zeros((2, 192, 576), np.float32)
    for block in range(6):
        for level in range(2):
            for row in range(4):
                for c in range(3):
                    at = block * 32 + beside_at(level, row, c)
                    table[level, at, block_row(block, row) * 24 + c] = 1
    return table


def grid_to_cells():
    table = np.zeros((384, 384), np.float32)
    for pr in range(2):
        for pc in range(2):
            for cw in range(2):
                for level in range(2):
                    for i in range(4):
                        for j in range(6):
                            at = (pr * 2 + pc) * 96 + cw * 48 + level * 24 + i * 6 + j
                            source = level * 192 + (2 * i + pr) * 24 + 2 * (6 * cw + j) + pc
                            table[at, source] = 1
    return table


def differences():
    token = np.arange(144)
    level = (token // 24) % 2
    low = ((token // 48) * 4 + (token % 24) // 6) >= 6
    keys = np.concatenate([token[:128], np.tile(token[128:], 8)])
    by_level = (level[:, None] != level[keys][None]).astype(np.float32)
    by_row = (low[:, None] != low[keys][None]).astype(np.float32)
    return np.stack([by_level, by_row]) * np.float32(-1e30)


def half_masks():
    left = np.zeros((2, 128, 128), np.float32)
    left[0, :, :64] = 1
    left[1, :, 64:] = 1
    return left


def tail_mask():
    return (np.arange(128)[:, None] // 16 == np.arange(512)[None] // 64).astype(np.float32)


def head_sums():
    at = np.arange(256) // 64
    return (at[:, None] == at[None]).astype(np.float32)


def norm_block(values, gain):
    mean = jnp.mean(values, axis=-1, keepdims=True)
    center = values - mean
    spread = jnp.mean(center * center, axis=-1, keepdims=True)
    return (center * lax.rsqrt(spread + 1e-05) * gain).astype(BF)


def head_scale(tau_ref, first):
    at = lax.broadcasted_iota(jnp.int32, (1, 256), 1) // 64
    scale = jnp.zeros((1, 256), F32)
    for h in range(4):
        scale = jnp.where(at == h, tau_ref[:, first + h : first + h + 1], scale)
    return scale * LOG2E


def make_qkv(x_ref, w_ref, q_ref, k_ref, v_ref, tau_ref, sums, width, group):
    def product(target, part, half):
        at = part * width + group * 512 + half * 256
        target[:, half * 256 : half * 256 + 256] = dot(x_ref[...], w_ref[:, at : at + 256]).astype(BF)

    def unit(target, half, scaled):
        lanes = slice(half * 256, half * 256 + 256)
        values = target[:, lanes]
        factor = lax.rsqrt(dot(values * values, sums) + 1e-06)
        if scaled:
            factor = factor * head_scale(tau_ref, group * 8 + half * 4)
        target[:, lanes] = (values.astype(F32) * factor).astype(BF)

    product(q_ref, 0, 0)
    product(q_ref, 0, 1)
    unit(q_ref, 0, True)
    product(k_ref, 1, 0)
    unit(q_ref, 1, True)
    product(k_ref, 1, 1)
    unit(k_ref, 0, False)
    product(v_ref, 2, 0)
    unit(k_ref, 1, False)
    product(v_ref, 2, 1)


def attend(
    q_ref, k_ref, v_ref, out_ref, out_at, bias_ref, masks_ref, tail_ref, weight_ref, windows
):
    left, right = masks_ref[0], masks_ref[1]
    tail = tail_ref[...]

    def weights(score, bias):
        return jnp.exp2(score if bias is None else score + bias).astype(BF)

    bias_main = bias_tail = None
    if bias_ref is not None:
        bias_main = jnp.concatenate([bias_ref[:, :128], bias_ref[:, :128]], axis=1)
        bias_tail = bias_ref[:, 128:]
    for w in range(windows):
        row = w * 144
        rows = slice(row, row + 144)
        q = q_ref[rows, :]
        k_tails = jnp.concatenate([k_ref[row + 128 : row + 144, :]] * 8, axis=0) * tail
        score = lax.dot_general(q, k_tails, NT, preferred_element_type=F32)
        weight_tail = weights(score, bias_tail)
        for pair in range(4):
            lanes = slice(pair * 128, pair * 128 + 128)
            k = k_ref[row : row + 128, lanes]
            k_pair = jnp.concatenate([k * left, k * right], axis=0)
            score = lax.dot_general(q[:, lanes], k_pair, NT, preferred_element_type=F32)
            weight_ref[rows, pair * 384 : pair * 384 + 256] = weights(score, bias_main)
            weight_ref[rows, pair * 384 + 256 : pair * 384 + 384] = weight_tail
    for w in range(windows):
        row = w * 144
        rows = slice(row, row + 144)
        v_tails = jnp.concatenate([v_ref[row + 128 : row + 144, :]] * 8, axis=0) * tail
        for pair in range(4):
            lanes = slice(pair * 128, pair * 128 + 128)
            v = v_ref[row : row + 128, lanes]
            v_pair = jnp.concatenate(
                [
                    jnp.concatenate([v * left, left], axis=1),
                    jnp.concatenate([v * right, right], axis=1),
                    jnp.concatenate([v_tails[:, lanes], tail[:, lanes]], axis=1),
                ],
                axis=0,
            )
            both = dot(weight_ref[rows, pair * 384 : pair * 384 + 384], v_pair)
            mixed = (both[:, :128] / both[:, 128:]).astype(BF)
            out_ref[rows, out_at + pair * 128 : out_at + pair * 128 + 128] = mixed


class Mover:
    def __init__(self, send_sem, recv_sem):
        self.send_sem, self.recv_sem = send_sem, recv_sem
        self.count = 0
        self.sent = []

    def send(self, source, target, device):
        copy = pltpu.make_async_remote_copy(
            src_ref=source,
            dst_ref=target,
            send_sem=self.send_sem.at[self.count],
            recv_sem=self.recv_sem.at[self.count],
            device_id=device,
            device_id_type=MESH,
        )
        copy.start()
        self.count += 1
        self.sent.append(copy)
        return copy

    def finish(self):
        for copy in self.sent:
            copy.wait_send()


class Place:
    def __init__(self, lat_size, lon_size):
        lat, lon = lax.axis_index("lat"), lax.axis_index("lon")
        self.lat, self.lon = lat, lon
        self.up, self.down = lax.rem(lat + lat_size - 1, lat_size), lax.rem(lat + 1, lat_size)
        self.west, self.east = lax.rem(lon + lon_size - 1, lon_size), lax.rem(lon + 1, lon_size)
        self.last = (lat == lat_size - 1).astype(F32)
        self.x_next, self.x_last = lax.rem(lon + 4, 16), lax.rem(lon + 12, 16)
        self.x_far = lax.rem(lon + 8, 16)
        self.mate = lon + 1 - 2 * lax.rem(lon, 2)
        self.across = lon + 2 - 4 * lax.rem(lon // 2, 2)
        self.z = lat // 2
        self.other_z = tuple(lax.rem(lat + 2 * n, 8) for n in (1, 3, 2))
        self.halo = (
            (self.up, lon),
            (self.down, lon),
            (lat, self.west),
            (lat, self.east),
            (self.up, self.west),
            (self.down, self.east),
        )
        self.gather = (
            (lat, self.x_next),
            (lat, self.x_last),
            (lat, self.mate),
            (lat, self.across),
        ) + tuple((other, lon) for other in self.other_z)


class Gather:
    def __init__(self, place, rows, columns, mover):
        self.place, self.rows, self.columns, self.mover = place, rows, columns, mover
        self.from_mate = []

    def part(self, owner, first, size):
        return self.rows.at[pl.ds(pl.multiple_of(owner * 64 + first, 16), size), self.columns]

    def send(self, owner, first, size, device):
        part = self.part(owner, first, size)
        return self.mover.send(part, part, device)

    def to_mate(self, owner):
        place = self.place
        self.from_mate.append(self.send(owner, 0, 64, (place.lat, place.mate)))

    def along_x(self, owner):
        place = self.place
        return (
            self.send(owner, 0, 64, (place.lat, place.x_next)),
            self.send(owner, 0, 64, (place.lat, place.x_last)),
        )

    def relay_x(self, before, after):
        place = self.place
        return (
            self.send(before, 0, 32, (place.lat, place.x_next)),
            self.send(after, 32, 32, (place.lat, place.x_last)),
        )

    def across_of(self, lon):
        return lon + 2 - 4 * lax.rem(lon // 2, 2)

    def send_quarter(self):
        place = self.place
        quarter = pl.multiple_of(place.z * 16, 16)
        self.quarter = self.send(place.lon, quarter, 16, (place.lat, place.across))

    def start(self):
        self.near = self.along_x(self.place.lon)
        self.to_mate(self.place.lon)

    def spread_quarter(self):
        place = self.place
        self.quarter.wait_recv()
        quarter = pl.multiple_of(place.z * 16, 16)
        self.quarters = [
            self.send(place.across, quarter, 16, (other, place.lon)) for other in place.other_z
        ]

    def second(self):
        place = self.place
        for copy in self.near:
            copy.wait_recv()
        self.far = self.relay_x(place.x_last, place.x_next)
        self.to_mate(place.x_last)
        self.to_mate(place.x_next)
        for copy in self.quarters:
            copy.wait_recv()
        self.near_across = self.along_x(place.across)
        self.to_mate(place.across)

    def third(self):
        for copy in self.far:
            copy.wait_recv()
        self.to_mate(self.place.x_far)

    def fourth(self):
        place = self.place
        for copy in self.near_across:
            copy.wait_recv()
        before, after = self.across_of(place.x_last), self.across_of(place.x_next)
        self.far_across = self.relay_x(before, after)
        self.to_mate(before)
        self.to_mate(after)

    def fifth(self):
        for copy in self.far_across:
            copy.wait_recv()
        self.to_mate(self.across_of(self.place.x_far))

    def finish(self):
        for copy in self.from_mate:
            copy.wait_recv()


class Fine:
    def __init__(self, grid, gain, wq, wp, tau, place, tables, work, comm, copy_sem):
        self.grid, self.gain, self.wq, self.wp, self.tau = grid, gain, wq, wp, tau
        self.place, self.tables, self.work = place, tables, work
        (
            self.blocks,
            self.picked,
            self.row_out,
            self.col_out,
            self.row_in,
            self.col_in,
            there_sems,
            back_sems,
        ) = comm
        self.there, self.back = Mover(*there_sems), Mover(*back_sems)
        self.copy_sem = copy_sem
        self.rows, self.columns, self.row_backs, self.col_backs = {}, {}, {}, {}
        self.own = []

    def send_rows(self, g, side):
        level, target = LEVELS[g][side], (self.place.up, self.place.lon)
        grid, blocks = self.grid, self.blocks
        self.rows[g, side] = (
            self.there.send(
                grid.at[level, pl.ds(0, 48)], blocks.at[g, 4, pl.ds(96 * side + 48, 48)], target
            ),
            self.there.send(
                grid.at[level, pl.ds(48, 96)], blocks.at[g, 5, pl.ds(96 * side, 96)], target
            ),
        )

    def send_columns(self, g):
        pick, grid = self.tables[3], self.grid
        picked, blocks, place = self.picked, self.blocks, self.place
        picks = dot(pick[0], grid[LEVELS[g][0]]) + dot(pick[1], grid[LEVELS[g][1]])
        for b in range(6):
            picked[g, b] = picks[32 * b : 32 * b + 32].astype(BF)
        beside, above = (place.lat, place.west), (place.up, place.west)
        send = self.there.send
        near, far = pl.ds(192, 16), pl.ds(208, 16)
        both = pl.ds(192, 32)
        self.columns[g] = (
            send(picked.at[g, pl.ds(0, 4)], blocks.at[g, pl.ds(0, 4), both], beside),
            send(picked.at[g, 4, pl.ds(0, 16)], blocks.at[g, 4, near], beside),
            send(picked.at[g, 4, pl.ds(16, 16)], blocks.at[g, 4, far], above),
            send(picked.at[g, 5], blocks.at[g, 5, both], above),
        )

    def place_own(self, g, side):
        level = LEVELS[g][side]
        for b in range(5):
            size = 96 if b < 4 else 48
            copy = pltpu.make_async_copy(
                self.grid.at[level, pl.ds(144 + 96 * b, size)],
                self.blocks.at[g, b, pl.ds(96 * side, size)],
                self.copy_sem.at[(g * 2 + side) * 5 + b],
            )
            copy.start()
            self.own.append(copy)

    def add_rows(self, level, at, size, values):
        grid = self.grid
        grid[level, pl.ds(at, size), :] = (
            grid[level, pl.ds(at, size), :].astype(F32) + values
        ).astype(BF)

    def wait_for(self, g, half):
        if half == 0:
            self.columns[g][0].wait_recv()
            return
        for copy in self.columns[g][1:] + self.rows[g, 0] + self.rows[g, 1]:
            copy.wait_recv()

    def unit(self, g, half):
        to_windows, from_windows, _, _, diff_ref, masks_ref, tail_ref, sums_ref = self.tables
        x_ref, q_ref, k_ref, v_ref, mixed_ref, shifted_ref, bias_ref, weight_ref = self.work
        for b in range(3):
            tokens_in = dot(to_windows[...], self.blocks[g, 3 * half + b])
            normed = norm_block(tokens_in, self.gain[...])
            for w in range(4):
                at = w * 144 + b * 48
                x_ref[at : at + 48, :] = normed[48 * w : 48 * w + 48]
        make_qkv(x_ref, self.wq, q_ref, k_ref, v_ref, self.tau, sums_ref[...], 512, 0)
        masked = g == 1 or half == 1
        if masked:
            bias = jnp.zeros((144, 256), F32)
            if g == 1:
                bias = bias + diff_ref[0]
            if half == 1:
                bias = bias + diff_ref[1] * self.place.last
            bias_ref[...] = bias
        attend(
            q_ref,
            k_ref,
            v_ref,
            mixed_ref,
            0,
            bias_ref if masked else None,
            masks_ref,
            tail_ref,
            weight_ref,
            4,
        )
        shifted_ref[...] = dot(mixed_ref[...], self.wp[...]).astype(BF)
        for b in range(3):
            index = 3 * half + b
            parts = [shifted_ref[w * 144 + b * 48 : w * 144 + b * 48 + 48, :] for w in range(4)]
            placed = dot(from_windows[...], jnp.concatenate(parts, axis=0))
            self.col_out[g, index] = placed[192:224].astype(BF)
            for side in range(2):
                level = LEVELS[g][side]
                mine = placed[96 * side : 96 * side + 96]
                if index < 4:
                    self.add_rows(level, 144 + 96 * index, 96, mine)
                elif index == 4:
                    self.add_rows(level, 528, 48, mine[:48])
                    self.row_out[g, 144 * side : 144 * side + 48, :] = mine[48:].astype(BF)
                else:
                    self.row_out[g, 144 * side + 48 : 144 * side + 144, :] = mine.astype(BF)

    def return_rows(self, g, side):
        part = pl.ds(144 * side, 144)
        self.row_backs[g, side] = self.back.send(
            self.row_out.at[g, part], self.row_in.at[g, part], (self.place.down, self.place.lon)
        )

    def return_columns(self, g):
        place, send = self.place, self.back.send
        beside, below = (place.lat, place.east), (place.down, place.east)

        def one(part, device):
            return send(self.col_out.at[(g, *part)], self.col_in.at[(g, *part)], device)

        self.col_backs[g] = (
            one((pl.ds(0, 4),), beside),
            one((4, pl.ds(0, 16)), beside),
            one((4, pl.ds(16, 16)), below),
            one((5,), below),
        )

    def take_columns(self, g):
        spread = self.tables[2]
        for copy in self.col_backs[g]:
            copy.wait_recv()
        for b in range(6):
            placed = dot(spread[...], self.col_in[g, b])
            for side in range(2):
                level, mine = LEVELS[g][side], placed[96 * side : 96 * side + 96]
                if b < 4:
                    self.add_rows(level, 144 + 96 * b, 96, mine)
                elif b == 4:
                    self.add_rows(level, 528, 48, mine[:48])
                    self.add_rows(level, 0, 48, mine[48:])
                else:
                    self.add_rows(level, 48, 96, mine)

    def take_rows(self, g, side):
        self.row_backs[g, side].wait_recv()
        above = self.row_in[g, 144 * side : 144 * side + 144, :].astype(F32)
        self.add_rows(LEVELS[g][side], 0, 144, above)

    def units(self, between):
        for copy in self.own:
            copy.wait()
        between[0]()
        self.unit(0, 0)
        between[1]()
        self.wait_for(0, 1)
        self.unit(0, 1)
        self.return_rows(0, 0)
        self.return_rows(0, 1)
        self.return_columns(0)
        between[2]()
        self.wait_for(1, 0)
        self.wait_for(1, 1)
        self.unit(1, 1)
        self.return_rows(1, 1)
        self.return_rows(1, 0)
        between[3]()
        self.unit(1, 0)
        self.return_columns(1)
        self.there.finish()


def merge_pass(g, grid, gains, wm, to_cells, merged, coarse, x_ref):
    merge_gain, gain = gains
    for b in range(3):
        cells = dot(to_cells[:, :192], grid[2 * g, pl.ds(192 * b, 192), :]) + dot(
            to_cells[:, 192:], grid[2 * g + 1, pl.ds(192 * b, 192), :]
        )
        parts = [cells[96 * n : 96 * n + 96] for n in range(4)]
        mean = sum(jnp.sum(part, axis=-1, keepdims=True) for part in parts) * (1 / 2048)
        parts = [part - mean for part in parts]
        spread = sum(jnp.sum(part * part, axis=-1, keepdims=True) for part in parts)
        factor = lax.rsqrt(spread * (1 / 2048) + 1e-05)
        for n in range(4):
            lanes = slice(512 * n, 512 * n + 512)
            normed = (parts[n] * factor * merge_gain[:, lanes]).astype(BF)
            for c in range(2):
                at = c * 144 + b * 48
                merged[at : at + 48, lanes] = normed[48 * c : 48 * c + 48]
    for n in range(4):
        lanes = slice(256 * n, 256 * n + 256)
        coarse[:, lanes] = dot(merged[...], wm[:, lanes]).astype(BF)
    for w in range(2):
        at = slice(144 * w, 144 * w + 144)
        x_ref[at, :] = norm_block(coarse[at, :].astype(F32), gain[...])


def coarse_pass(g, grid, weights, tau, tables, work, loaded, gather_proj):
    wc, ws = weights
    from_cells, masks_ref, tail_ref, sums_ref = tables
    coarse, x_ref, q_ref, k_ref, v_ref, mixed_ref, split, weight_ref = work
    for group in range(2):
        make_qkv(x_ref, wc, q_ref, k_ref, v_ref, tau, sums_ref[...], 1024, group)
        attend(
            q_ref,
            k_ref,
            v_ref,
            mixed_ref,
            group * 512,
            None,
            masks_ref,
            tail_ref,
            weight_ref,
            2,
        )
    if g == 0:
        gather_proj.finish()
    for n in range(4):
        lanes = slice(256 * n, 256 * n + 256)
        update = dot(mixed_ref[...], wc[:, 3072 + 256 * n : 3328 + 256 * n])
        coarse[:, lanes] = (coarse[:, lanes].astype(F32) + update).astype(BF)
    if g == 0:
        loaded.wait()
    for n in range(8):
        lanes = slice(256 * n, 256 * n + 256)
        split[:, lanes] = dot(coarse[...], ws[:, lanes]).astype(BF)
    for b in range(3):
        parts = []
        for n in range(4):
            for c in range(2):
                at = c * 144 + b * 48
                parts.append(split[at : at + 48, 512 * n : 512 * n + 512])
        placed = dot(from_cells[...], jnp.concatenate(parts, axis=0))
        for side in range(2):
            here = grid.at[2 * g + side, pl.ds(192 * b, 192)]
            here[...] = (here[...].astype(F32) + placed[192 * side : 192 * side + 192]).astype(BF)


SCRATCH = {
    "grid": ((4, 576, 512), BF),
    "blocks": ((2, 6, 224, 512), BF),
    "picked": ((2, 6, 32, 512), BF),
    "row_out": ((2, 288, 512), BF),
    "col_out": ((2, 6, 32, 512), BF),
    "row_in": ((2, 288, 512), BF),
    "col_in": ((2, 6, 32, 512), BF),
    "x_fine": ((576, 512), BF),
    "q": ((576, 512), BF),
    "k": ((576, 512), BF),
    "v": ((576, 512), BF),
    "mixed_fine": ((576, 512), BF),
    "shifted": ((576, 512), BF),
    "bias": ((144, 256), F32),
    "merged": ((288, 2048), BF),
    "coarse": ((2, 288, 1024), BF),
    "x_coarse": ((2, 288, 1024), BF),
    "mixed_coarse": ((288, 1024), BF),
    "split": ((288, 2048), BF),
    "attention": ((576, 1536), BF),
    "coarse_weights": ((1024, 4096), BF),
}
SEMAPHORES = {
    "load": 40,
    "copy": 20,
    "there_send": 16,
    "there_recv": 16,
    "back_send": 12,
    "back_recv": 12,
    "gather_send": 40,
    "gather_recv": 40,
}


def kernel(lat_size, lon_size, names, *refs):
    count = len(names)
    given = dict(zip(names, refs[:count]))
    out = refs[count]
    held = dict(zip(names[3:], refs[count + 1 :]))
    rest = refs[count + 1 + count - 3 :]
    at = dict(zip(list(SCRATCH) + list(SEMAPHORES), rest))
    place = Place(lat_size, lon_size)
    grid, whole = at["grid"], at["coarse_weights"]
    start = pl.ds(pl.multiple_of(place.lon * 64, 16), 64)
    loads = {}

    def load(name, source, target):
        loads[name] = pltpu.make_async_copy(source, target, at["load"].at[len(loads)])
        loads[name].start()

    load("tokens", given["tokens"], grid)
    load("coarse_qkv", given["coarse_qkv"], whole.at[start, pl.ds(0, 3072)])
    load("coarse_proj", given["coarse_proj"], whole.at[start, pl.ds(3072, 1024)])
    for name in names[3:]:
        load(name, given[name], held[name])

    barrier = pltpu.get_barrier_semaphore()
    partners = place.halo + place.gather
    for device in partners:
        pl.semaphore_signal(barrier, inc=1, device_id=device, device_id_type=MESH)
    pl.semaphore_wait(barrier, len(partners))

    mover = Mover(at["gather_send"], at["gather_recv"])
    gather_qkv = Gather(place, whole, pl.ds(0, 3072), mover)
    gather_proj = Gather(place, whole, pl.ds(3072, 1024), mover)
    late = ("merge_weight", "expand_weight")
    loads["tokens"].wait()

    fine_tables = [
        held[name]
        for name in ("windows", "windows_t", "spread", "pick", "differ", "masks", "tail", "sums")
    ]
    work = [
        at[name]
        for name in ("x_fine", "q", "k", "v", "mixed_fine", "shifted", "bias", "attention")
    ]
    comm = [at[name] for name in ("blocks", "picked", "row_out", "col_out", "row_in", "col_in")]
    comm += [(at["there_send"], at["there_recv"]), (at["back_send"], at["back_recv"])]

    def fine(prefix):
        return Fine(
            grid,
            held[prefix + "_gain"],
            held[prefix + "_qkv"],
            held[prefix + "_proj"],
            held[prefix + "_tau"],
            place,
            fine_tables,
            work,
            comm,
            at["copy"],
        )

    def merge(g):
        merge_pass(
            g,
            grid,
            (held["merge_gain"], held["coarse_gain"]),
            held["merge_weight"],
            held["cells"],
            at["merged"],
            at["coarse"].at[g],
            at["x_coarse"].at[g],
        )

    def coarse(g):
        half = pl.ds(0, 288)
        coarse_pass(
            g,
            grid,
            (whole, held["expand_weight"]),
            held["coarse_tau"],
            [held[name] for name in ("cells_t", "masks", "tail", "sums")],
            [at[name].at[g] for name in ("coarse", "x_coarse")]
            + [at[name].at[half] for name in ("q", "k", "v")]
            + [at[name] for name in ("mixed_coarse", "split", "attention")],
            loads["expand_weight"],
            gather_proj,
        )

    first = fine("enc")
    loads["coarse_qkv"].wait()
    gather_qkv.send_quarter()
    first.send_rows(0, 0)
    first.send_rows(0, 1)
    for g in range(2):
        for side in range(2):
            first.place_own(g, side)
    loads["pick"].wait()
    first.send_columns(0)
    gather_qkv.start()
    first.send_columns(1)
    for name in ("coarse_proj",) + names[3:]:
        if name not in late + ("pick",) and not name.startswith("dec_"):
            loads[name].wait()

    def before_first():
        first.wait_for(0, 0)
        first.send_rows(1, 1)
        first.send_rows(1, 0)
        gather_qkv.spread_quarter()

    def after_second():
        gather_qkv.third()
        gather_proj.send_quarter()
        gather_proj.start()

    def after_third():
        gather_qkv.fourth()
        gather_proj.spread_quarter()

    first.units((before_first, gather_qkv.second, after_second, after_third))
    gather_qkv.fifth()
    gather_proj.second()
    first.take_columns(0)
    first.take_columns(1)
    first.take_rows(0, 0)
    first.take_rows(0, 1)
    first.take_rows(1, 1)
    loads["merge_weight"].wait()
    gather_proj.third()
    merge(0)
    gather_proj.fourth()
    first.take_rows(1, 0)
    first.back.finish()
    merge(1)
    gather_proj.fifth()
    gather_qkv.finish()
    coarse(0)
    second = fine("dec")
    for name in ("dec_gain", "dec_tau", "dec_qkv", "dec_proj"):
        loads[name].wait()
    second.send_rows(0, 0)
    second.send_rows(1, 1)
    second.place_own(0, 0)
    second.place_own(1, 1)
    coarse(1)
    second.send_rows(0, 1)
    second.send_columns(0)
    second.send_columns(1)
    second.send_rows(1, 0)
    second.place_own(0, 1)
    second.place_own(1, 0)
    mover.finish()
    nothing = lambda: None
    second.units((lambda: second.wait_for(0, 0), nothing, nothing, nothing))
    for g in range(2):
        second.take_columns(g)
        for side in range(2):
            second.take_rows(g, side)
    second.back.finish()
    store = pltpu.make_async_copy(grid, out, at["load"].at[0])
    store.start()
    store.wait()


def publish_kernel(source, target, held, load_sem, store_sem):
    loads, stores = [], []
    for level in range(4):
        for part in range(2):
            rows, at = pl.ds(288 * part, 288), level * 2 + part
            here = held.at[level, rows]
            loads.append(pltpu.make_async_copy(source.at[level, rows], here, load_sem.at[at]))
            stores.append(pltpu.make_async_copy(here, target.at[level, rows], store_sem.at[at]))
            loads[-1].start()
    for load, store in zip(loads, stores):
        load.wait()
        store.start()
    for store in stores:
        store.wait()


def publish(values):
    return pl.pallas_call(
        publish_kernel,
        out_shape=jax.ShapeDtypeStruct(values.shape, values.dtype),
        in_specs=[HBM],
        out_specs=HBM,
        scratch_shapes=[
            pltpu.VMEM(values.shape, values.dtype),
            pltpu.SemaphoreType.DMA((8,)),
            pltpu.SemaphoreType.DMA((8,)),
        ],
        compiler_params=pltpu.CompilerParams(vmem_limit_bytes=60 << 20),
        name="publish",
    )(values)


def local(
    tokens,
    enc_gain,
    enc_qkv,
    enc_proj,
    enc_tau,
    merge_gain,
    merge_weight,
    coarse_gain,
    coarse_qkv,
    coarse_proj,
    coarse_tau,
    expand_weight,
    dec_gain,
    dec_qkv,
    dec_proj,
    dec_tau,
):
    table = lambda values: jnp.asarray(values, BF)
    row = lambda values: values.reshape(1, -1)
    windows, cells = block_to_windows(), grid_to_cells()
    given = {
        "tokens": tokens.reshape(4, 576, 512),
        "coarse_qkv": coarse_qkv,
        "coarse_proj": coarse_proj,
        "enc_gain": row(enc_gain),
        "enc_tau": row(enc_tau),
        "pick": table(grid_to_beside()),
        "windows": table(windows),
        "enc_qkv": enc_qkv,
        "sums": table(head_sums()),
        "masks": table(half_masks()),
        "tail": table(tail_mask()),
        "enc_proj": enc_proj,
        "windows_t": table(windows.T),
        "spread": table(beside_to_block()),
        "differ": jnp.asarray(differences()),
        "merge_gain": row(merge_gain),
        "coarse_gain": row(coarse_gain),
        "coarse_tau": row(coarse_tau),
        "dec_gain": row(dec_gain),
        "dec_tau": row(dec_tau),
        "dec_qkv": dec_qkv,
        "dec_proj": dec_proj,
        "cells": table(cells),
        "cells_t": table(cells.T),
        "merge_weight": merge_weight,
        "expand_weight": expand_weight,
    }
    names = tuple(given)
    scratch = [pltpu.VMEM(given[name].shape, given[name].dtype) for name in names[3:]]
    scratch += [pltpu.VMEM(shape, dtype) for shape, dtype in SCRATCH.values()]
    scratch += [pltpu.SemaphoreType.DMA((n,)) for n in SEMAPHORES.values()]
    decoded = pl.pallas_call(
        functools.partial(kernel, lax.axis_size("lat"), lax.axis_size("lon"), names),
        out_shape=jax.ShapeDtypeStruct((4, 576, 512), BF),
        in_specs=[HBM] * len(names),
        out_specs=HBM,
        scratch_shapes=scratch,
        compiler_params=pltpu.CompilerParams(
            collective_id=0, has_side_effects=True, vmem_limit_bytes=60 << 20
        ),
        cost_estimate=pl.CostEstimate(
            flops=35_000_000_000, bytes_accessed=30_000_000, transcendentals=8_000_000
        ),
        name="blocks",
    )(*given.values())
    return publish(decoded).reshape(4, 24, 24, 512)


def solution(mesh):
    placed = (
        P(None, "lat", "lon", None),
        P(),
        P(),
        P(),
        P(),
        P(),
        P(),
        P(),
        P("lon", None),
        P("lon", None),
        P(),
        P(),
        P(),
        P(),
        P(),
        P(),
    )
    return jax.shard_map(
        local, mesh=mesh, in_specs=placed, out_specs=P(None, "lat", "lon", None), check_vma=False
    )
```
